32 devices in a mesh: pair: 2 (over core), ctx: 4 (over y, x), vocab: 4 (over z).
Axes of the slice: x: 2, y: 2, z: 4, core: 2. Of those that a mesh axis runs over, the one named last changes fastest.
Arguments:
- hidden: bfloat16 [2, 512, 8192], P('pair', 'ctx'), may hold values from -8 to 8
- head_weight: bfloat16 [8192, 8192], P(('ctx', 'vocab'), 'pair'), may hold values from -2 to 2
- labels: int32 [2, 512], P('pair'), may hold values from 0 to 8191
- token_mask: int32 [2, 512], P('pair'), may hold values 0 or 1
- other_logps: float32 [2], P('pair'), may hold values from -780300 to -780000
- ref_logps: float32 [2], P('pair'), may hold values from -781300 to -781000
Outputs:
- grad_hidden: bfloat16 [2, 512, 8192], P(None, 'ctx', ('pair', 'vocab'))
- grad_head: bfloat16 [8192, 8192], P(('ctx', 'vocab'), 'pair')
The draws below stay inside these ranges and needn't reach their ends.
All inputs are finite; a program needn't handle non-finite values. No bound on the sum of `token_mask` on one device may be relied on, other than what follows from the above.
Results may differ from the reference program's by a relative error of at most 0.012.
Values may be sent and summed in bfloat16 or wider, within the bound.
A program may use at most 128 MiB of HBM per device.

```python
import math
import jax
import jax.numpy as jnp

D = 8192
TOK = 512
V = 8192


def head_table(key):
    normal_draw = jax.random.normal(jax.random.fold_in(key, 7), (V, D), jnp.float32)
    return jnp.clip(normal_draw, -4.0, 4.0) * (3.0 / math.sqrt(D))


def draw_head_weight(key, part):
    return head_table(key).astype(jnp.bfloat16)


def draw_hidden(key, part):
    base = jnp.clip(jax.random.normal(jax.random.fold_in(key, 11), (2, TOK, D), jnp.float32), -6.0, 6.0)
    return jnp.clip(base, -8.0, 8.0).astype(jnp.bfloat16)


def set_ends(drawn, rng, smallest, top_value):
    longest = drawn.shape.index(max(drawn.shape))
    spots = []
    for shift in (0, 1):
        where = [jax.random.randint(jax.random.fold_in(rng, axis), (), 0, length) for axis, length in enumerate(drawn.shape)]
        where[longest] = (where[longest] + shift) % drawn.shape[longest]
        spots.append(tuple(where))
    return drawn.at[spots[0]].set(smallest).at[spots[1]].set(top_value)


def level_of(rng, extent, cuts, least, largest):
    loudness = 1.0
    for dim, parts in cuts:
        steps = jax.random.uniform(jax.random.fold_in(jax.random.fold_in(rng, 6), dim), (parts,), jnp.float32, least / len(cuts), largest / len(cuts))
        loudness = loudness * jnp.repeat(jnp.exp(steps), extent[dim] // parts).reshape((-1,) + (1,) * (len(extent) - 1 - dim))
    return loudness


def setup_inputs(seed: int = 0) -> dict:
    keys = jax.random.split(jax.random.key(seed), 7)
    hidden = draw_hidden(jax.random.fold_in(keys[6], 71), 0)
    head_weight = draw_head_weight(jax.random.fold_in(keys[6], 71), 0)
    labels = set_ends(jax.random.randint(keys[2], (2, TOK), 0, V), jax.random.fold_in(keys[2], 1), 0, V - 1).astype(jnp.int32)
    token_mask = set_ends((jax.random.randint(keys[3], (2, TOK), 0, 4) < 3).astype(jnp.int32), jax.random.fold_in(keys[3], 1), 0, 1)
    other_logps = jnp.clip(-780300.0 + 300.0 * jax.random.uniform(keys[4], (2,), jnp.float32) ** level_of(keys[4], (2,), ((0, 2),), -0.2, 0.2), -780300.0, -780000.0)
    ref_logps = jnp.clip(-781300.0 + 300.0 * jax.random.uniform(keys[5], (2,), jnp.float32) ** level_of(keys[5], (2,), ((0, 2),), -0.2, 0.2), -781300.0, -781000.0)
    return {"hidden": hidden, "head_weight": head_weight, "labels": labels, "token_mask": token_mask, "other_logps": other_logps, "ref_logps": ref_logps}


beta_value = 0.01
z_weight = 0.0001
loss_scale = 4096.0


def reference(hidden, head_weight, labels, token_mask, other_logps, ref_logps):
    logit_list = []
    total_list = []
    label_list = []
    for member in range(2):
        logits = jnp.dot(hidden[member], head_weight.T, preferred_element_type=jnp.float32)
        row_max = jnp.max(logits, axis=1)
        log_total = row_max + jnp.log(jnp.sum(jnp.exp(logits - row_max[:, None]), axis=1))
        label_logit = jnp.take_along_axis(logits, labels[member][:, None], axis=1)[:, 0]
        logit_list.append(logits)
        total_list.append(log_total)
        label_list.append(label_logit)
    maskf = token_mask.astype(jnp.float32)
    relative = []
    for member in range(2):
        slice_sum = jnp.sum(maskf[member] * (label_list[member] - total_list[member]))
        relative.append((slice_sum + other_logps[member]) - ref_logps[member])
    margin = beta_value * (relative[0] - relative[1])
    coef = beta_value * jax.nn.sigmoid(-margin)
    seq_coefs = [-coef, coef]
    columns = jnp.arange(head_weight.shape[0], dtype=jnp.int32)
    grads_hidden = []
    grad_head = jnp.zeros(head_weight.shape, jnp.float32)
    for member in range(2):
        logits = logit_list[member]
        log_total = total_list[member]
        probs = jnp.exp(logits - log_total[:, None])
        onehot = (labels[member][:, None] == columns[None, :]).astype(jnp.float32)
        logit_grad = (loss_scale * maskf[member][:, None] * (seq_coefs[member] * (onehot - probs) + 2.0 * z_weight * log_total[:, None] * probs)).astype(jnp.bfloat16)
        grads_hidden.append(jnp.dot(logit_grad, head_weight, preferred_element_type=jnp.float32).astype(jnp.bfloat16))
        grad_head = grad_head + jnp.dot(logit_grad.T, hidden[member], preferred_element_type=jnp.float32)
    return jnp.stack(grads_hidden, axis=0), grad_head.astype(jnp.bfloat16)
```

```python
import functools

import jax
import jax.numpy as jnp
from jax import lax
from jax.experimental import pallas as pl
from jax.experimental.pallas import tpu as pltpu
from jax.sharding import PartitionSpec as P

beta_value = 0.01
z_weight = 0.0001
loss_scale = 4096.0
F32, BF16 = jnp.float32, jnp.bfloat16
PARTS = 4


def flip(index, mask):
    bit = 1
    while bit <= mask:
        if mask & bit:
            index = index + bit * (1 - 2 * lax.rem(lax.div(index, bit), 2))
        bit *= 2
    return index


def kernel(
    n, hid, w_hbm, lab_in, msk_in, oth_in, ref_in, gh_out, head_out,
    w, H, LT, LR, GT, G, S1, R1, S2, R2, ZS, ZR, FA, HO, GO, st, st2, zst, cst, auxi, auxf,
    lsem, psem, aux_sem, ag_s, ag_r, lt_s, lt_r, zst_s, zst_r, cst_s, cst_r,
    s1_s, s1_r, s2_s, s2_r, z_s, z_r, ho_sem,
):
    p, c, z = lax.axis_index("pair"), lax.axis_index("ctx"), lax.axis_index("vocab")
    q = 1 - p
    partner = (q, c, z)
    tl = H.shape[2]
    half = w.shape[1]
    rows = w.shape[0]
    m = n // PARTS
    cw = half // n
    CW = half // PARTS
    ktile = 512

    def at_ctx(d):
        return (p, flip(c, d), z)

    def at_vocab(x):
        return (p, c, flip(z, x))

    def remote(src, dst, ss, rs, dev):
        return pltpu.make_async_remote_copy(
            src_ref=src, dst_ref=dst, send_sem=ss, recv_sem=rs,
            device_id=dev, device_id_type=pl.DeviceIdType.MESH,
        )

    cp_w = pltpu.make_async_copy(w_hbm, w, lsem.at[0])
    cp_w.start()
    own_cols = pl.ds(pl.multiple_of(p * half, half), half)
    other_cols = pl.ds(pl.multiple_of(q * half, half), half)
    cp_h = pltpu.make_async_copy(hid.at[0, :, own_cols], H.at[0, p], lsem.at[1])
    cp_h.start()
    auxi[p, 0:1, :] = lab_in[...]
    auxi[p, 1:2, :] = msk_in[...]
    auxf[p, 0:1, :] = jnp.broadcast_to(oth_in[...], (1, 128))
    auxf[p, 1:2, :] = jnp.broadcast_to(ref_in[...], (1, 128))

    barrier = pltpu.get_barrier_semaphore()
    peers = [partner] + [at_ctx(d) for d in (1, 2, 3)] + [at_vocab(x) for x in range(1, n)]
    for dev in peers:
        pl.semaphore_signal(barrier, inc=1, device_id=dev, device_id_type=pl.DeviceIdType.MESH)
    pl.semaphore_wait(barrier, len(peers))

    to_partner = remote(hid.at[0, :, other_cols], H.at[0, p], psem.at[0], psem.at[1], partner)
    to_partner.start()
    ag = []
    for d in (1, 2):
        cp = remote(hid.at[0, :, own_cols], H.at[d, p], ag_s.at[d, p], ag_r.at[d, p], at_ctx(d))
        cp.start()
        ag.append(cp)
    ax = [
        remote(auxi.at[p], auxi.at[p], aux_sem.at[0], aux_sem.at[1], partner),
        remote(auxf.at[p], auxf.at[p], aux_sem.at[2], aux_sem.at[3], partner),
    ]
    for cp in ax:
        cp.start()
    to_partner.wait_recv()
    for d in (1, 2):
        cp = remote(H.at[0, q], H.at[d, q], ag_s.at[d, q], ag_r.at[d, q], at_ctx(d))
        cp.start()
        ag.append(cp)
    cp_w.wait()
    cp_h.wait()

    def ag_wait(d, s):
        remote(H.at[d, s], H.at[d, s], ag_s.at[d, s], ag_r.at[d, s], at_ctx(d)).wait_recv()

    lt_copies = []

    def logits(d):
        LT[d] = jnp.zeros((rows, 2 * tl), F32)

        def body(k, carry):
            cols = pl.ds(pl.multiple_of(k * ktile, ktile), ktile)
            block = H[d, :, :, cols].reshape(2 * tl, ktile)
            LT[d] += lax.dot_general(
                w[:, cols], block, (((1,), (1,)), ((), ())), preferred_element_type=F32
            )
            return carry

        lax.fori_loop(0, half // ktile, body, 0)
        cp = remote(LT.at[d], LR.at[d], lt_s.at[d], lt_r.at[d], partner)
        cp.start()
        lt_copies.append(cp)

    base = (c * n + z) * rows

    def is_label(d, s):
        toks = pl.ds(pl.multiple_of(flip(c, d) * tl, tl), tl)
        return lax.broadcasted_iota(jnp.int32, (rows, tl), 0) == auxi[s, 0:1, toks] - base

    def local_stats(d):
        lt_copies[d].wait()
        for s in range(2):
            lanes = slice(s * tl, (s + 1) * tl)
            l = LT[d, :, lanes] + LR[d, :, lanes]
            top = jnp.max(l, axis=0, keepdims=True)
            e = jnp.exp(l - top)
            LT[d, :, lanes] = e
            st[d, s, 0:1, :] = top
            st[d, s, 1:2, :] = jnp.sum(e, axis=0, keepdims=True)
            st[d, s, 2:3, :] = jnp.sum(jnp.where(is_label(d, s), l, 0.0), axis=0, keepdims=True)

    logits(0)
    ag_wait(1, 0)
    fwd0 = remote(H.at[1, 0], H.at[3, 0], ag_s.at[3, 0], ag_r.at[3, 0], at_ctx(2))
    fwd0.start()
    ag_wait(2, 1)
    fwd1 = remote(H.at[2, 1], H.at[3, 1], ag_s.at[3, 1], ag_r.at[3, 1], at_ctx(1))
    fwd1.start()
    for cp in ax:
        cp.wait()
    ag_wait(1, 1)
    logits(1)
    ag_wait(2, 0)
    logits(2)
    local_stats(0)
    local_stats(1)
    local_stats(2)
    ag_wait(3, 0)
    ag_wait(3, 1)
    logits(3)
    local_stats(3)

    zc = []
    for x in range(1, n):
        cp = remote(st, zst.at[x], zst_s.at[x], zst_r.at[x], at_vocab(x))
        cp.start()
        zc.append(cp)
    for cp in zc:
        cp.wait()

    def merge(parts):
        top = functools.reduce(jnp.maximum, [t for t, _, _ in parts])
        total = sum(s * jnp.exp(t - top) for t, s, _ in parts)
        label = sum(l for _, _, l in parts)
        return top, total, label

    def read(ref, *at):
        return tuple(ref[(*at, slice(r, r + 1), slice(None))] for r in range(3))

    for d in range(4):
        for s in range(2):
            got = merge([read(st, d, s)] + [read(zst, x, d, s) for x in range(1, n)])
            for r in range(3):
                st2[d, s, r : r + 1, :] = got[r]
    cc = []
    for k in (3, 1, 2):
        cp = remote(st2, cst.at[k], cst_s.at[k], cst_r.at[k], at_ctx(k))
        cp.start()
        cc.append(cp)
    for cp in cc:
        cp.wait()
    log_total, maskf = {}, {}
    relative = []
    for s in range(2):
        acc = jnp.zeros((1, tl), F32)
        for d in range(4):
            top, total, label = merge(
                [read(st2, d, s)] + [read(cst, k, k ^ d, s) for k in (1, 2, 3)]
            )
            lt = top + jnp.log(total)
            toks = pl.ds(pl.multiple_of(flip(c, d) * tl, tl), tl)
            mk = auxi[s, 1:2, toks].astype(F32)
            log_total[d, s], maskf[d, s] = lt, mk
            acc = acc + mk * (label - lt)
        slice_sum = jnp.sum(acc, axis=1, keepdims=True)
        relative.append((slice_sum + auxf[s, 0:1, 0:1]) - auxf[s, 1:2, 0:1])
    margin = beta_value * (relative[0] - relative[1])
    coef = beta_value / (1.0 + jnp.exp(margin))

    for d in (3, 1, 2, 0):
        for s in range(2):
            seq = coef if s == 1 else -coef
            lanes = slice(s * tl, (s + 1) * tl)
            lt, mk = log_total[d, s], maskf[d, s]
            b = loss_scale * mk * seq
            a = loss_scale * mk * (2.0 * z_weight * lt - seq) * jnp.exp(st[d, s, 0:1, :] - lt)
            g = LT[d, :, lanes] * a + jnp.where(is_label(d, s), b, 0.0)
            GT[d, :, lanes] = g.astype(BF16)
            G[d, s] = g.T.astype(BF16)

    zs = lax.div(z, m)
    first, second = (1, 2), (2, 1)

    def cols(i):
        return pl.ds(pl.multiple_of(flip(zs, PARTS - 1 - i) * CW, CW), CW)

    def term(d, s, i):
        return jnp.dot(G[d, s], w[:, cols(i)], preferred_element_type=F32)

    c1, c2, cz = {}, {}, []

    def send_first(i):
        for s in range(2):
            f = first[s]
            S1[i, s, 1] = term(3, s, i).astype(BF16)
            S1[i, s, 0] = term(f, s, i).astype(BF16)
            c1[i, s] = remote(S1.at[i, s], R1.at[i, s], s1_s.at[i, s], s1_r.at[i, s], at_ctx(f))
            c1[i, s].start()

    def send_second(i):
        for s in range(2):
            g = second[s]
            mine = term(g, s, i)
            c1[i, s].wait_recv()
            S2[i, s] = (mine + R1[i, s, 1].astype(F32)).astype(BF16)
            c2[i, s] = remote(S2.at[i, s], R2.at[i, s], s2_s.at[i, s], s2_r.at[i, s], at_ctx(g))
            c2[i, s].start()

    def send_vocab(i):
        for s in range(2):
            mine = term(0, s, i) + R1[i, s, 0].astype(F32)
            c2[i, s].wait_recv()
            mine = mine + R2[i, s].astype(F32)
            if i == PARTS - 1:
                FA[s] = mine
            ZS[i, s] = mine.astype(BF16)
        zm = lax.rem(z, m)
        for k in reversed(range(m)):
            x = (PARTS - 1 - i) * m + k
            if x == 0:
                continue
            if m == 1:
                src = ZS.at[i]
            else:
                src = ZS.at[i, :, :, pl.ds(pl.multiple_of(flip(zm, k) * cw, cw), cw)]
            cp = remote(src, ZR.at[x], z_s.at[x], z_r.at[x], at_vocab(x))
            cp.start()
            cz.append(cp)

    tile = 512
    head_tiles = half // tile

    def head_copy(t):
        where = pl.ds(pl.multiple_of(t * tile, tile), tile)
        return pltpu.make_async_copy(HO.at[:, where], head_out.at[:, where], ho_sem.at[t])

    def head(low, high):
        def body(t, carry):
            where = pl.ds(pl.multiple_of(t * tile, tile), tile)
            acc = jnp.zeros((rows, tile), F32)
            for d in range(4):
                acc += jnp.dot(
                    GT[d], H[d, :, :, where].reshape(2 * tl, tile), preferred_element_type=F32
                )
            HO[:, where] = acc.astype(BF16)
            head_copy(t).start()
            return carry

        lax.fori_loop(low, high, body, 0)

    send_first(0)
    send_first(1)
    head(0, head_tiles // 2)
    send_second(0)
    send_first(2)
    head(head_tiles // 2, head_tiles)
    send_second(1)
    send_vocab(0)
    send_first(3)
    send_second(2)
    send_vocab(1)
    send_second(3)
    send_vocab(2)
    send_vocab(3)
    zm = lax.rem(z, m)
    own = pl.ds(0, cw) if m == 1 else pl.ds(pl.multiple_of(zm * cw, cw), cw)
    for cp in cz:
        cp.wait_recv()
    for s in range(2):
        total = FA[s, :, own]
        for x in range(1, n):
            total = total + ZR[x, s].astype(F32)
        GO[s] = total.astype(BF16)
    out = pltpu.make_async_copy(GO, gh_out, lsem.at[2])
    out.start()
    to_partner.wait_send()
    for cp in ag + [fwd0, fwd1]:
        cp.wait_send()
    for cp in list(c1.values()) + list(c2.values()) + cz:
        cp.wait_send()

    def drain(t, carry):
        head_copy(t).wait()
        return carry

    lax.fori_loop(0, head_tiles, drain, 0)
    out.wait()


def solution(mesh):
    n = mesh.shape["vocab"]

    def local(hidden, head_weight, labels, token_mask, other_logps, ref_logps):
        tl = hidden.shape[1]
        rows, half = head_weight.shape
        toks = labels.shape[1]
        CW, cw = half // PARTS, half // n
        vm = pltpu.VMEM
        dma = pltpu.SemaphoreType.DMA
        any_spec = pl.BlockSpec(memory_space=pl.ANY)
        vmem_spec = pl.BlockSpec(memory_space=pltpu.VMEM)
        return pl.pallas_call(
            functools.partial(kernel, n),
            out_shape=(
                jax.ShapeDtypeStruct((2, tl, cw), BF16),
                jax.ShapeDtypeStruct((rows, half), BF16),
            ),
            in_specs=[any_spec, any_spec] + [vmem_spec] * 4,
            out_specs=(any_spec, any_spec),
            scratch_shapes=[
                vm((rows, half), BF16),
                vm((4, 2, tl, half), BF16),
                vm((4, rows, 2 * tl), F32),
                vm((4, rows, 2 * tl), F32),
                vm((4, rows, 2 * tl), BF16),
                vm((4, 2, tl, rows), BF16),
                vm((PARTS, 2, 2, tl, CW), BF16),
                vm((PARTS, 2, 2, tl, CW), BF16),
                vm((PARTS, 2, tl, CW), BF16),
                vm((PARTS, 2, tl, CW), BF16),
                vm((PARTS, 2, tl, CW), BF16),
                vm((n, 2, tl, cw), BF16),
                vm((2, tl, CW), F32),
                vm((rows, half), BF16),
                vm((2, tl, cw), BF16),
                vm((4, 2, 8, tl), F32),
                vm((4, 2, 8, tl), F32),
                vm((n, 4, 2, 8, tl), F32),
                vm((4, 4, 2, 8, tl), F32),
                vm((2, 8, toks), jnp.int32),
                vm((2, 8, 128), F32),
                dma((3,)),
                dma((2,)),
                dma((4,)),
                dma((4, 2)),
                dma((4, 2)),
                dma((4,)),
                dma((4,)),
                dma((n,)),
                dma((n,)),
                dma((4,)),
                dma((4,)),
                dma((PARTS, 2)),
                dma((PARTS, 2)),
                dma((PARTS, 2)),
                dma((PARTS, 2)),
                dma((n,)),
                dma((n,)),
                dma((half // 512,)),
            ],
            compiler_params=pltpu.CompilerParams(
                collective_id=0, has_side_effects=True, vmem_limit_bytes=58 * 1024 * 1024
            ),
            cost_estimate=pl.CostEstimate(
                flops=6 * 8 * tl * rows * half, bytes_accessed=6 * rows * half, transcendentals=0
            ),
        )(
            hidden, head_weight, labels, token_mask,
            other_logps.reshape(1, 1), ref_logps.reshape(1, 1),
        )

    return jax.shard_map(
        local,
        mesh=mesh,
        in_specs=(
            P("pair", "ctx", None),
            P(("ctx", "vocab"), "pair"),
            P("pair", None),
            P("pair", None),
            P("pair"),
            P("pair"),
        ),
        out_specs=(P(None, "ctx", ("pair", "vocab")), P(("ctx", "vocab"), "pair")),
        check_vma=False,
    )
```

```python
import functools

import jax
import jax.numpy as jnp
from jax import lax
from jax.experimental import pallas as pl
from jax.experimental.pallas import tpu as pltpu
from jax.sharding import PartitionSpec as P

beta_value = 0.01
z_weight = 0.0001
loss_scale = 4096.0
F32, BF16 = jnp.float32, jnp.bfloat16
PARTS = 4


def flip(index, mask):
    bit = 1
    while bit <= mask:
        if mask & bit:
            index = index + bit * (1 - 2 * lax.rem(lax.div(index, bit), 2))
        bit *= 2
    return index


def kernel(
    n, hid, w_hbm, lab_in, msk_in, oth_in, ref_in, gh_out, head_out,
    w, H, LT, LR, GT, G, S1, R1, S2, R2, ZS, ZR, FA, HO, GO, st, st2, zst, cst, ab, auxi, auxf,
    lsem, psem, aux_sem, az_s, az_r, ag_s, ag_r, ch_s, ch_r, lt_s, lt_r, zst_s, zst_r, cst_s, cst_r,
    s1_s, s1_r, s2_s, s2_r, z_s, z_r, ho_sem,
):
    p, c, z = lax.axis_index("pair"), lax.axis_index("ctx"), lax.axis_index("vocab")
    q = 1 - p
    partner = (q, c, z)
    tl = H.shape[2]
    half = w.shape[1]
    rows = w.shape[0]
    m = n // PARTS
    cw = half // n
    CW = half // PARTS
    ktile = 512
    zs = lax.div(z, m)
    zq = half * 3 // (8 * PARTS)
    rest = slice(zq * PARTS, half)
    hr = tl // 2

    def at_ctx(d):
        return (p, flip(c, d), z)

    def at_vocab(x):
        return (p, c, flip(z, x))

    def remote(src, dst, ss, rs, dev):
        return pltpu.make_async_remote_copy(
            src_ref=src, dst_ref=dst, send_sem=ss, recv_sem=rs,
            device_id=dev, device_id_type=pl.DeviceIdType.MESH,
        )

    cp_w = pltpu.make_async_copy(w_hbm, w, lsem.at[0])
    cp_w.start()
    own_cols = pl.ds(pl.multiple_of(p * half, half), half)
    other_cols = pl.ds(pl.multiple_of(q * half, half), half)
    cp_h = pltpu.make_async_copy(hid.at[0, :, own_cols], H.at[0, p], lsem.at[1])
    cp_h.start()
    auxi[p, 0:1, :] = lab_in[...]
    auxi[p, 1:2, :] = msk_in[...]
    auxf[p, 0:1, :] = jnp.broadcast_to(oth_in[...], (1, 128))
    auxf[p, 1:2, :] = jnp.broadcast_to(ref_in[...], (1, 128))

    barrier = pltpu.get_barrier_semaphore()
    peers = [partner] + [at_ctx(d) for d in (1, 2, 3)] + [at_vocab(x) for x in range(1, n)]
    for dev in peers:
        pl.semaphore_signal(barrier, inc=1, device_id=dev, device_id_type=pl.DeviceIdType.MESH)
    pl.semaphore_wait(barrier, len(peers))

    to_partner = remote(hid.at[0, :, other_cols], H.at[0, p], psem.at[0], psem.at[1], partner)
    to_partner.start()
    ag = []

    def zcols(k):
        return pl.ds(pl.multiple_of(k * zq, zq), zq)

    def send_z(d, s, src, to, into):
        cp = remote(src, H.at[into, s, :, zcols(zs)], az_s.at[into, s], az_r.at[into, s], at_ctx(to))
        cp.start()
        ag.append(cp)

    def send_rest(h, s, src, to, into):
        cp = remote(
            src, H.at[into, s, h * hr : (h + 1) * hr, rest],
            ag_s.at[into, s, h], ag_r.at[into, s, h], at_ctx(to),
        )
        cp.start()
        ag.append(cp)

    def own_rest(h):
        where = pl.ds(pl.multiple_of(p * half + zq * PARTS, 128), half - zq * PARTS)
        return hid.at[0, h * hr : (h + 1) * hr, where]

    def held_rest(d, s, h):
        return H.at[d, s, h * hr : (h + 1) * hr, rest]

    own_z = hid.at[0, :, pl.ds(pl.multiple_of(p * half + zs * zq, 128), zq)]
    for d in (1, 2):
        send_z(0, p, own_z, d, d)
    for d in (1, 2):
        send_rest(0, p, own_rest(0), d, d)
    ax = [
        remote(auxi.at[p], auxi.at[p], aux_sem.at[0], aux_sem.at[1], partner),
        remote(auxf.at[p], auxf.at[p], aux_sem.at[2], aux_sem.at[3], partner),
    ]
    for cp in ax:
        cp.start()
    to_partner.wait_recv()
    for d in (1, 2):
        send_z(0, q, H.at[0, q, :, zcols(zs)], d, d)
    for d in (1, 2):
        send_rest(1, p, own_rest(1), d, d)

    def z_wait(d, s):
        part = H.at[d, s, :, zcols(zs)]
        remote(part, part, az_s.at[d, s], az_r.at[d, s], at_ctx(d)).wait_recv()

    def rest_wait(d, s):
        for h in range(2):
            part = held_rest(d, s, h)
            remote(part, part, ag_s.at[d, s, h], ag_r.at[d, s, h], at_ctx(d)).wait_recv()

    def chain_copy(way, j, d, part):
        piece = H.at[d, :, :, zcols(part)]
        dev = (p, c, lax.rem(z + n + (m if way == 0 else -m), n))
        return remote(piece, piece, ch_s.at[way, j, d], ch_r.at[way, j, d], dev)

    def chain_sent(way, j):
        part = zs - j if way == 0 else zs + j
        if way == 0:
            return part, jnp.logical_and(zs < PARTS - 1, part >= 0)
        return part, jnp.logical_and(zs > 0, part < PARTS)

    def chain_send(j, blocks):
        for d in blocks:
            for way in range(2):
                part, there = chain_sent(way, j)

                @pl.when(there)
                def _():
                    chain_copy(way, j, d, part).start()

    def chain_wait_send(j, d):
        for way in range(2):
            part, there = chain_sent(way, j)

            @pl.when(there)
            def _():
                chain_copy(way, j, d, part).wait_send()

    def chain_recv(j, blocks):
        for d in blocks:
            for way in range(2):
                part = zs - 1 - j if way == 0 else zs + 1 + j

                @pl.when(part >= 0 if way == 0 else part < PARTS)
                def _():
                    chain_copy(way, j, d, part).wait_recv()

    z_wait(1, 0)
    send_z(1, 0, H.at[1, 0, :, zcols(zs)], 2, 3)
    z_wait(2, 1)
    send_z(2, 1, H.at[2, 1, :, zcols(zs)], 1, 3)
    for h in range(2):
        for d in (1, 2):
            send_rest(h, q, held_rest(0, q, h), d, d)
    z_wait(1, 1)
    z_wait(2, 0)
    chain_send(0, (1, 2))
    cp_w.wait()
    cp_h.wait()

    lt_copies = []

    def logits(d):
        LT[d] = jnp.zeros((rows, 2 * tl), F32)

        def body(k, carry):
            cols = pl.ds(pl.multiple_of(k * ktile, ktile), ktile)
            block = H[d, :, :, cols].reshape(2 * tl, ktile)
            LT[d] += lax.dot_general(
                w[:, cols], block, (((1,), (1,)), ((), ())), preferred_element_type=F32
            )
            return carry

        lax.fori_loop(0, half // ktile, body, 0)
        cp = remote(LT.at[d], LR.at[d], lt_s.at[d], lt_r.at[d], partner)
        cp.start()
        lt_copies.append(cp)

    base = (c * n + z) * rows

    def is_label(d, s):
        toks = pl.ds(pl.multiple_of(flip(c, d) * tl, tl), tl)
        return lax.broadcasted_iota(jnp.int32, (rows, tl), 0) == auxi[s, 0:1, toks] - base

    def local_stats(d):
        lt_copies[d].wait()
        for s in range(2):
            u = 2 * d + s
            lanes = slice(s * tl, (s + 1) * tl)
            l = LT[d, :, lanes] + LR[d, :, lanes]
            top = jnp.max(l, axis=0, keepdims=True)
            e = jnp.exp(l - top)
            LT[d, :, lanes] = e
            st[0, u : u + 1, :] = top
            st[1, u : u + 1, :] = jnp.sum(e, axis=0, keepdims=True)
            st[2, u : u + 1, :] = jnp.sum(
                jnp.where(is_label(d, s), l, 0.0), axis=0, keepdims=True
            )

    logits(0)
    z_wait(3, 0)
    z_wait(3, 1)
    chain_send(0, (3,))
    chain_recv(0, (1, 2))
    chain_send(1, (1, 2))
    chain_recv(0, (3,))
    chain_send(1, (3,))
    for cp in ax:
        cp.wait()
    local_stats(0)
    chain_recv(1, (1, 2))
    chain_send(2, (1, 2))
    rest_wait(1, 0)
    for h in range(2):
        send_rest(h, 0, held_rest(1, 0, h), 2, 3)
    rest_wait(2, 1)
    for h in range(2):
        send_rest(h, 1, held_rest(2, 1, h), 1, 3)
    chain_recv(1, (3,))
    chain_send(2, (3,))
    rest_wait(1, 1)
    rest_wait(2, 0)
    chain_recv(2, (1, 2))
    logits(1)
    logits(2)
    local_stats(1)
    local_stats(2)
    chain_recv(2, (3,))
    rest_wait(3, 0)
    rest_wait(3, 1)
    logits(3)
    local_stats(3)

    zc = []
    for x in range(1, n):
        cp = remote(st, zst.at[x], zst_s.at[x], zst_r.at[x], at_vocab(x))
        cp.start()
        zc.append(cp)
    for cp in zc:
        cp.wait()

    def merge(parts):
        top = functools.reduce(jnp.maximum, [t for t, _, _ in parts])
        total = sum(s * jnp.exp(t - top) for t, s, _ in parts)
        label = sum(l for _, _, l in parts)
        return top, total, label

    def read(ref, *at):
        return tuple(ref[(*at, r)] for r in range(3))

    got = merge([read(st)] + [read(zst, x) for x in range(1, n)])
    for r in range(3):
        st2[r] = got[r]
    cc = []
    for k in (3, 1, 2):
        cp = remote(st2, cst.at[k], cst_s.at[k], cst_r.at[k], at_ctx(k))
        cp.start()
        cc.append(cp)
    for cp in cc:
        cp.wait()

    def read_ctx(k):
        return tuple(
            jnp.concatenate(
                [cst[k, r, 2 * (k ^ d) : 2 * (k ^ d) + 2, :] for d in range(4)], axis=0
            )
            for r in range(3)
        )

    top, total, label = merge([got] + [read_ctx(k) for k in (1, 2, 3)])
    lt = top + jnp.log(total)
    mask_rows = []
    for d in range(4):
        toks = pl.ds(pl.multiple_of(flip(c, d) * tl, tl), tl)
        mask_rows += [auxi[0, 1:2, toks], auxi[1, 1:2, toks]]
    mk = jnp.concatenate(mask_rows, axis=0).astype(F32)
    response = lax.rem(lax.broadcasted_iota(jnp.int32, (8, tl), 0), 2)
    counted = mk * (label - lt)
    relative = []
    for s in range(2):
        part = jnp.sum(jnp.where(response == s, counted, 0.0), axis=0, keepdims=True)
        slice_sum = jnp.sum(part, axis=1, keepdims=True)
        relative.append((slice_sum + auxf[s, 0:1, 0:1]) - auxf[s, 1:2, 0:1])
    margin = beta_value * (relative[0] - relative[1])
    coef = beta_value / (1.0 + jnp.exp(margin))
    seq = jnp.where(response == 1, coef, -coef)
    ab[0] = loss_scale * mk * (2.0 * z_weight * lt - seq) * jnp.exp(st[0] - lt)
    ab[1] = loss_scale * mk * seq

    def gradient(d, s):
        u = 2 * d + s
        lanes = slice(s * tl, (s + 1) * tl)
        b = jnp.where(is_label(d, s), ab[1, u : u + 1, :], 0.0)
        g = LT[d, :, lanes] * ab[0, u : u + 1, :] + b
        GT[d, :, lanes] = g.astype(BF16)
        G[d, s] = g.T.astype(BF16)

    first, second = (1, 2), (2, 1)

    def cols(i):
        return pl.ds(pl.multiple_of(flip(zs, PARTS - 1 - i) * CW, CW), CW)

    def term(d, s, i):
        return jnp.dot(G[d, s], w[:, cols(i)], preferred_element_type=F32)

    c1, c2, cz = {}, {}, []
    second_term, own_term = {}, {}

    def send_first(i, h):
        hs = slice(h * hr, (h + 1) * hr)
        for s in range(2):
            f = first[s]
            if h == 0:
                S1[i, s, 1] = term(3, s, i).astype(BF16)
                S1[i, s, 0] = term(f, s, i).astype(BF16)
            cp = remote(
                S1.at[i, s, :, hs], R1.at[i, s, :, hs],
                s1_s.at[i, s, h], s1_r.at[i, s, h], at_ctx(f),
            )
            cp.start()
            c1[i, s, h] = cp

    def send_second(i, h):
        hs = slice(h * hr, (h + 1) * hr)
        for s in range(2):
            g = second[s]
            if h == 0:
                second_term[s] = term(g, s, i)
            c1[i, s, h].wait_recv()
            S2[i, s, hs] = (second_term[s][hs] + R1[i, s, 1, hs].astype(F32)).astype(BF16)
            cp = remote(
                S2.at[i, s, hs], R2.at[i, s, hs], s2_s.at[i, s, h], s2_r.at[i, s, h], at_ctx(g)
            )
            cp.start()
            c2[i, s, h] = cp

    zm = lax.rem(z, m)

    def send_vocab(i, h):
        hs = slice(h * hr, (h + 1) * hr)
        for s in range(2):
            if h == 0:
                own_term[s] = term(0, s, i)
            mine = own_term[s][hs] + R1[i, s, 0, hs].astype(F32)
            c2[i, s, h].wait_recv()
            mine = mine + R2[i, s, hs].astype(F32)
            if i == PARTS - 1:
                FA[s, hs] = mine
            ZS[i, s, hs] = mine.astype(BF16)
        for k in reversed(range(m)):
            x = (PARTS - 1 - i) * m + k
            if x == 0:
                continue
            if m == 1:
                src = ZS.at[i, :, hs]
            else:
                src = ZS.at[i, :, hs, pl.ds(pl.multiple_of(flip(zm, k) * cw, cw), cw)]
            cp = remote(src, ZR.at[x, :, hs], z_s.at[x, h], z_r.at[x, h], at_vocab(x))
            cp.start()
            cz.append(cp)

    tile = 512
    head_tiles = half // tile

    def head_copy(t):
        where = pl.ds(pl.multiple_of(t * tile, tile), tile)
        return pltpu.make_async_copy(HO.at[:, where], head_out.at[:, where], ho_sem.at[t])

    def head(low, high):
        def body(t, carry):
            where = pl.ds(pl.multiple_of(t * tile, tile), tile)
            acc = jnp.zeros((rows, tile), F32)
            for d in range(4):
                acc += jnp.dot(
                    GT[d], H[d, :, :, where].reshape(2 * tl, tile), preferred_element_type=F32
                )
            HO[:, where] = acc.astype(BF16)
            head_copy(t).start()
            return carry

        lax.fori_loop(low, high, body, 0)

    for d, s in ((3, 0), (1, 0), (3, 1), (2, 1)):
        gradient(d, s)
    send_first(0, 0)
    send_first(0, 1)
    for d, s in ((2, 0), (1, 1), (0, 0), (0, 1)):
        gradient(d, s)
    send_first(1, 0)
    head(0, 1)
    send_second(0, 0)
    send_first(1, 1)
    head(1, 2)
    send_second(0, 1)
    send_first(2, 0)
    head(2, 3)
    send_second(1, 0)
    send_vocab(0, 0)
    send_first(2, 1)
    head(3, 4)
    send_second(1, 1)
    send_vocab(0, 1)
    send_first(3, 0)
    head(4, 5)
    send_second(2, 0)
    send_vocab(1, 0)
    send_first(3, 1)
    head(5, 6)
    send_second(2, 1)
    send_vocab(1, 1)
    head(6, 7)
    send_second(3, 0)
    send_vocab(2, 0)
    head(7, head_tiles)
    send_second(3, 1)
    send_vocab(2, 1)
    send_vocab(3, 0)
    send_vocab(3, 1)
    own = pl.ds(0, cw) if m == 1 else pl.ds(pl.multiple_of(zm * cw, cw), cw)
    for cp in cz:
        cp.wait_recv()
    for s in range(2):
        total = FA[s, :, own]
        for x in range(1, n):
            total = total + ZR[x, s].astype(F32)
        GO[s] = total.astype(BF16)
    out = pltpu.make_async_copy(GO, gh_out, lsem.at[2])
    out.start()
    to_partner.wait_send()
    for cp in ag:
        cp.wait_send()
    for j in range(3):
        for d in (1, 2, 3):
            chain_wait_send(j, d)
    for cp in list(c1.values()) + list(c2.values()) + cz:
        cp.wait_send()

    def drain(t, carry):
        head_copy(t).wait()
        return carry

    lax.fori_loop(0, head_tiles, drain, 0)
    out.wait()


def solution(mesh):
    n = mesh.shape["vocab"]

    def local(hidden, head_weight, labels, token_mask, other_logps, ref_logps):
        tl = hidden.shape[1]
        rows, half = head_weight.shape
        toks = labels.shape[1]
        CW, cw = half // PARTS, half // n
        vm = pltpu.VMEM
        dma = pltpu.SemaphoreType.DMA
        any_spec = pl.BlockSpec(memory_space=pl.ANY)
        vmem_spec = pl.BlockSpec(memory_space=pltpu.VMEM)
        return pl.pallas_call(
            functools.partial(kernel, n),
            out_shape=(
                jax.ShapeDtypeStruct((2, tl, cw), BF16),
                jax.ShapeDtypeStruct((rows, half), BF16),
            ),
            in_specs=[any_spec, any_spec] + [vmem_spec] * 4,
            out_specs=(any_spec, any_spec),
            scratch_shapes=[
                vm((rows, half), BF16),
                vm((4, 2, tl, half), BF16),
                vm((4, rows, 2 * tl), F32),
                vm((4, rows, 2 * tl), F32),
                vm((4, rows, 2 * tl), BF16),
                vm((4, 2, tl, rows), BF16),
                vm((PARTS, 2, 2, tl, CW), BF16),
                vm((PARTS, 2, 2, tl, CW), BF16),
                vm((PARTS, 2, tl, CW), BF16),
                vm((PARTS, 2, tl, CW), BF16),
                vm((PARTS, 2, tl, CW), BF16),
                vm((n, 2, tl, cw), BF16),
                vm((2, tl, CW), F32),
                vm((rows, half), BF16),
                vm((2, tl, cw), BF16),
                vm((3, 8, tl), F32),
                vm((3, 8, tl), F32),
                vm((n, 3, 8, tl), F32),
                vm((4, 3, 8, tl), F32),
                vm((2, 8, tl), F32),
                vm((2, 8, toks), jnp.int32),
                vm((2, 8, 128), F32),
                dma((3,)),
                dma((2,)),
                dma((4,)),
                dma((4, 2)),
                dma((4, 2)),
                dma((4, 2, 2)),
                dma((4, 2, 2)),
                dma((2, 3, 4)),
                dma((2, 3, 4)),
                dma((4,)),
                dma((4,)),
                dma((n,)),
                dma((n,)),
                dma((4,)),
                dma((4,)),
                dma((PARTS, 2, 2)),
                dma((PARTS, 2, 2)),
                dma((PARTS, 2, 2)),
                dma((PARTS, 2, 2)),
                dma((n, 2)),
                dma((n, 2)),
                dma((half // 512,)),
            ],
            compiler_params=pltpu.CompilerParams(
                collective_id=0, has_side_effects=True, vmem_limit_bytes=58 * 1024 * 1024
            ),
            cost_estimate=pl.CostEstimate(
                flops=6 * 8 * tl * rows * half, bytes_accessed=6 * rows * half, transcendentals=0
            ),
        )(
            hidden, head_weight, labels, token_mask,
            other_logps.reshape(1, 1), ref_logps.reshape(1, 1),
        )

    return jax.shard_map(
        local,
        mesh=mesh,
        in_specs=(
            P("pair", "ctx", None),
            P(("ctx", "vocab"), "pair"),
            P("pair", None),
            P("pair", None),
            P("pair"),
            P("pair"),
        ),
        out_specs=(P(None, "ctx", ("pair", "vocab")), P(("ctx", "vocab"), "pair")),
        check_vma=False,
    )
```

```python
import functools

import jax
import jax.numpy as jnp
from jax import lax
from jax.experimental import pallas as pl
from jax.experimental.pallas import tpu as pltpu
from jax.sharding import PartitionSpec as P

beta_value = 0.01
z_weight = 0.0001
loss_scale = 4096.0
F32, BF16 = jnp.float32, jnp.bfloat16
PARTS = 4


def flip(index, mask):
    bit = 1
    while bit <= mask:
        if mask & bit:
            index = index + bit * (1 - 2 * lax.rem(lax.div(index, bit), 2))
        bit *= 2
    return index


def kernel(
    n, hid, w_hbm, lab_in, msk_in, oth_in, ref_in, gh_out, head_out,
    w, H, LT, LR, GT, G, S1, R1, S2, R2, ZS, ZR, FA, HO, GO, st, st2, zst, cst, ab, auxi, auxf,
    lsem, psem, aux_sem, az_s, az_r, ag_s, ag_r, ch_s, ch_r, lt_s, lt_r, zst_s, zst_r, cst_s, cst_r,
    s1_s, s1_r, s2_s, s2_r, z_s, z_r, ho_sem,
):
    p, c, z = lax.axis_index("pair"), lax.axis_index("ctx"), lax.axis_index("vocab")
    q = 1 - p
    partner = (q, c, z)
    tl = H.shape[2]
    half = w.shape[1]
    rows = w.shape[0]
    m = n // PARTS
    cw = half // n
    CW = half // PARTS
    ktile = 512
    zs = lax.div(z, m)
    zq = half * 3 // (8 * PARTS)
    rest = slice(zq * PARTS, half)
    hr = tl // 2

    def at_ctx(d):
        return (p, flip(c, d), z)

    def at_vocab(x):
        return (p, c, flip(z, x))

    def remote(src, dst, ss, rs, dev):
        return pltpu.make_async_remote_copy(
            src_ref=src, dst_ref=dst, send_sem=ss, recv_sem=rs,
            device_id=dev, device_id_type=pl.DeviceIdType.MESH,
        )

    cp_w = pltpu.make_async_copy(w_hbm, w, lsem.at[0])
    cp_w.start()
    own_cols = pl.ds(pl.multiple_of(p * half, half), half)
    other_cols = pl.ds(pl.multiple_of(q * half, half), half)
    cp_h = pltpu.make_async_copy(hid.at[0, :, own_cols], H.at[0, p], lsem.at[1])
    cp_h.start()
    auxi[p, 0:1, :] = lab_in[...]
    auxi[p, 1:2, :] = msk_in[...]
    auxf[p, 0:1, :] = jnp.broadcast_to(oth_in[...], (1, 128))
    auxf[p, 1:2, :] = jnp.broadcast_to(ref_in[...], (1, 128))

    barrier = pltpu.get_barrier_semaphore()
    peers = [partner] + [at_ctx(d) for d in (1, 2, 3)] + [at_vocab(x) for x in range(1, n)]
    for dev in peers:
        pl.semaphore_signal(barrier, inc=1, device_id=dev, device_id_type=pl.DeviceIdType.MESH)
    pl.semaphore_wait(barrier, len(peers))

    to_partner = remote(hid.at[0, :, other_cols], H.at[0, p], psem.at[0], psem.at[1], partner)
    to_partner.start()
    ag = []

    def zcols(k):
        return pl.ds(pl.multiple_of(k * zq, zq), zq)

    def send_z(d, s, src, to, into):
        cp = remote(src, H.at[into, s, :, zcols(zs)], az_s.at[into, s], az_r.at[into, s], at_ctx(to))
        cp.start()
        ag.append(cp)

    def send_rest(h, s, src, to, into):
        cp = remote(
            src, H.at[into, s, h * hr : (h + 1) * hr, rest],
            ag_s.at[into, s, h], ag_r.at[into, s, h], at_ctx(to),
        )
        cp.start()
        ag.append(cp)

    def own_rest(h):
        where = pl.ds(pl.multiple_of(p * half + zq * PARTS, 128), half - zq * PARTS)
        return hid.at[0, h * hr : (h + 1) * hr, where]

    def held_rest(d, s, h):
        return H.at[d, s, h * hr : (h + 1) * hr, rest]

    own_z = hid.at[0, :, pl.ds(pl.multiple_of(p * half + zs * zq, 128), zq)]
    for d in (1, 2):
        send_z(0, p, own_z, d, d)
    for d in (1, 2):
        send_rest(0, p, own_rest(0), d, d)
    ax = [
        remote(auxi.at[p], auxi.at[p], aux_sem.at[0], aux_sem.at[1], partner),
        remote(auxf.at[p], auxf.at[p], aux_sem.at[2], aux_sem.at[3], partner),
    ]
    for cp in ax:
        cp.start()
    to_partner.wait_recv()
    for d in (1, 2):
        send_z(0, q, H.at[0, q, :, zcols(zs)], d, d)
    for d in (1, 2):
        send_rest(1, p, own_rest(1), d, d)

    def z_wait(d, s):
        part = H.at[d, s, :, zcols(zs)]
        remote(part, part, az_s.at[d, s], az_r.at[d, s], at_ctx(d)).wait_recv()

    def rest_wait(d, s):
        for h in range(2):
            part = held_rest(d, s, h)
            remote(part, part, ag_s.at[d, s, h], ag_r.at[d, s, h], at_ctx(d)).wait_recv()

    def chain_copy(way, j, d, part):
        piece = H.at[d, :, :, zcols(part)]
        dev = (p, c, lax.rem(z + n + (m if way == 0 else -m), n))
        return remote(piece, piece, ch_s.at[way, j, d], ch_r.at[way, j, d], dev)

    def chain_sent(way, j):
        part = zs - j if way == 0 else zs + j
        if way == 0:
            return part, jnp.logical_and(zs < PARTS - 1, part >= 0)
        return part, jnp.logical_and(zs > 0, part < PARTS)

    def chain_send(j, blocks):
        for d in blocks:
            for way in range(2):
                part, there = chain_sent(way, j)

                @pl.when(there)
                def _():
                    chain_copy(way, j, d, part).start()

    def chain_wait_send(j, d):
        for way in range(2):
            part, there = chain_sent(way, j)

            @pl.when(there)
            def _():
                chain_copy(way, j, d, part).wait_send()

    def chain_recv(j, blocks):
        for d in blocks:
            for way in range(2):
                part = zs - 1 - j if way == 0 else zs + 1 + j

                @pl.when(part >= 0 if way == 0 else part < PARTS)
                def _():
                    chain_copy(way, j, d, part).wait_recv()

    z_wait(1, 0)
    send_z(1, 0, H.at[1, 0, :, zcols(zs)], 2, 3)
    z_wait(2, 1)
    send_z(2, 1, H.at[2, 1, :, zcols(zs)], 1, 3)
    for h in range(2):
        for d in (1, 2):
            send_rest(h, q, held_rest(0, q, h), d, d)
    z_wait(1, 1)
    z_wait(2, 0)
    chain_send(0, (1, 2))
    cp_w.wait()
    cp_h.wait()

    lt_copies = []

    def add_logits(d, low, high):
        def body(k, carry):
            cols = pl.ds(pl.multiple_of(k * ktile, ktile), ktile)
            block = H[d, :, :, cols].reshape(2 * tl, ktile)
            LT[d] += lax.dot_general(
                w[:, cols], block, (((1,), (1,)), ((), ())), preferred_element_type=F32
            )
            return carry

        lax.fori_loop(low // ktile, high // ktile, body, 0)

    def swap_logits(d):
        cp = remote(LT.at[d], LR.at[d], lt_s.at[d], lt_r.at[d], partner)
        cp.start()
        lt_copies.append(cp)

    chained = zq * PARTS

    base = (c * n + z) * rows

    def is_label(d, s):
        toks = pl.ds(pl.multiple_of(flip(c, d) * tl, tl), tl)
        return lax.broadcasted_iota(jnp.int32, (rows, tl), 0) == auxi[s, 0:1, toks] - base

    def local_stats(d):
        lt_copies[d].wait()
        for s in range(2):
            u = 2 * d + s
            lanes = slice(s * tl, (s + 1) * tl)
            l = LT[d, :, lanes] + LR[d, :, lanes]
            top = jnp.max(l, axis=0, keepdims=True)
            e = jnp.exp(l - top)
            LT[d, :, lanes] = e
            st[0, u : u + 1, :] = top
            st[1, u : u + 1, :] = jnp.sum(e, axis=0, keepdims=True)
            st[2, u : u + 1, :] = jnp.sum(
                jnp.where(is_label(d, s), l, 0.0), axis=0, keepdims=True
            )

    for d in range(4):
        LT[d] = jnp.zeros((rows, 2 * tl), F32)
    add_logits(0, 0, half)
    swap_logits(0)
    z_wait(3, 0)
    z_wait(3, 1)
    chain_send(0, (3,))
    chain_recv(0, (1, 2))
    chain_send(1, (1, 2))
    chain_recv(0, (3,))
    chain_send(1, (3,))
    for cp in ax:
        cp.wait()
    local_stats(0)
    chain_recv(1, (1, 2))
    chain_send(2, (1, 2))
    rest_wait(1, 0)
    for h in range(2):
        send_rest(h, 0, held_rest(1, 0, h), 2, 3)
    rest_wait(2, 1)
    for h in range(2):
        send_rest(h, 1, held_rest(2, 1, h), 1, 3)
    chain_recv(1, (3,))
    chain_send(2, (3,))
    rest_wait(1, 1)
    rest_wait(2, 0)
    add_logits(1, chained, half)
    add_logits(2, chained, half)
    chain_recv(2, (1, 2))
    add_logits(1, 0, chained)
    swap_logits(1)
    add_logits(2, 0, chained)
    swap_logits(2)
    local_stats(1)
    chain_recv(2, (3,))
    add_logits(3, 0, chained)
    rest_wait(3, 0)
    rest_wait(3, 1)
    add_logits(3, chained, half)
    swap_logits(3)
    local_stats(2)
    local_stats(3)

    zc = []
    for x in range(1, n):
        cp = remote(st, zst.at[x], zst_s.at[x], zst_r.at[x], at_vocab(x))
        cp.start()
        zc.append(cp)
    for cp in zc:
        cp.wait()

    def merge(parts):
        top = functools.reduce(jnp.maximum, [t for t, _, _ in parts])
        total = sum(s * jnp.exp(t - top) for t, s, _ in parts)
        label = sum(l for _, _, l in parts)
        return top, total, label

    def read(ref, *at):
        return tuple(ref[(*at, r)] for r in range(3))

    got = merge([read(st)] + [read(zst, x) for x in range(1, n)])
    for r in range(3):
        st2[r] = got[r]
    cc = []
    for k in (3, 1, 2):
        cp = remote(st2, cst.at[k], cst_s.at[k], cst_r.at[k], at_ctx(k))
        cp.start()
        cc.append(cp)
    for cp in cc:
        cp.wait()

    def read_ctx(k):
        return tuple(
            jnp.concatenate(
                [cst[k, r, 2 * (k ^ d) : 2 * (k ^ d) + 2, :] for d in range(4)], axis=0
            )
            for r in range(3)
        )

    top, total, label = merge([got] + [read_ctx(k) for k in (1, 2, 3)])
    lt = top + jnp.log(total)
    mask_rows = []
    for d in range(4):
        toks = pl.ds(pl.multiple_of(flip(c, d) * tl, tl), tl)
        mask_rows += [auxi[0, 1:2, toks], auxi[1, 1:2, toks]]
    mk = jnp.concatenate(mask_rows, axis=0).astype(F32)
    response = lax.rem(lax.broadcasted_iota(jnp.int32, (8, tl), 0), 2)
    counted = mk * (label - lt)
    relative = []
    for s in range(2):
        part = jnp.sum(jnp.where(response == s, counted, 0.0), axis=0, keepdims=True)
        slice_sum = jnp.sum(part, axis=1, keepdims=True)
        relative.append((slice_sum + auxf[s, 0:1, 0:1]) - auxf[s, 1:2, 0:1])
    margin = beta_value * (relative[0] - relative[1])
    coef = beta_value / (1.0 + jnp.exp(margin))
    seq = jnp.where(response == 1, coef, -coef)
    ab[0] = loss_scale * mk * (2.0 * z_weight * lt - seq) * jnp.exp(st[0] - lt)
    ab[1] = loss_scale * mk * seq

    def gradient(d, s):
        u = 2 * d + s
        lanes = slice(s * tl, (s + 1) * tl)
        b = jnp.where(is_label(d, s), ab[1, u : u + 1, :], 0.0)
        g = LT[d, :, lanes] * ab[0, u : u + 1, :] + b
        GT[d, :, lanes] = g.astype(BF16)
        G[d, s] = g.T.astype(BF16)

    first, second = (1, 2), (2, 1)

    def cols(i):
        return pl.ds(pl.multiple_of(flip(zs, PARTS - 1 - i) * CW, CW), CW)

    def term(d, s, i):
        return jnp.dot(G[d, s], w[:, cols(i)], preferred_element_type=F32)

    c1, c2, cz = {}, {}, []
    second_term, own_term = {}, {}

    def send_first(i, h, responses=(0, 1)):
        hs = slice(h * hr, (h + 1) * hr)
        for s in responses:
            f = first[s]
            if h == 0:
                S1[i, s, 1] = term(3, s, i).astype(BF16)
                S1[i, s, 0] = term(f, s, i).astype(BF16)
            cp = remote(
                S1.at[i, s, :, hs], R1.at[i, s, :, hs],
                s1_s.at[i, s, h], s1_r.at[i, s, h], at_ctx(f),
            )
            cp.start()
            c1[i, s, h] = cp

    def send_second(i, h):
        hs = slice(h * hr, (h + 1) * hr)
        for s in range(2):
            g = second[s]
            if h == 0:
                second_term[s] = term(g, s, i)
            c1[i, s, h].wait_recv()
            S2[i, s, hs] = (second_term[s][hs] + R1[i, s, 1, hs].astype(F32)).astype(BF16)
            cp = remote(
                S2.at[i, s, hs], R2.at[i, s, hs], s2_s.at[i, s, h], s2_r.at[i, s, h], at_ctx(g)
            )
            cp.start()
            c2[i, s, h] = cp

    zm = lax.rem(z, m)

    def send_vocab(i, h):
        hs = slice(h * hr, (h + 1) * hr)
        for s in range(2):
            if h == 0:
                own_term[s] = term(0, s, i)
            mine = own_term[s][hs] + R1[i, s, 0, hs].astype(F32)
            c2[i, s, h].wait_recv()
            mine = mine + R2[i, s, hs].astype(F32)
            if i == PARTS - 1:
                FA[s, hs] = mine
            ZS[i, s, hs] = mine.astype(BF16)
        for k in reversed(range(m)):
            x = (PARTS - 1 - i) * m + k
            if x == 0:
                continue
            if m == 1:
                src = ZS.at[i, :, hs]
            else:
                src = ZS.at[i, :, hs, pl.ds(pl.multiple_of(flip(zm, k) * cw, cw), cw)]
            cp = remote(src, ZR.at[x, :, hs], z_s.at[x, h], z_r.at[x, h], at_vocab(x))
            cp.start()
            cz.append(cp)

    tile = 512
    head_tiles = half // tile

    def head_copy(t):
        where = pl.ds(pl.multiple_of(t * tile, tile), tile)
        return pltpu.make_async_copy(HO.at[:, where], head_out.at[:, where], ho_sem.at[t])

    def head(low, high):
        def body(t, carry):
            where = pl.ds(pl.multiple_of(t * tile, tile), tile)
            acc = jnp.zeros((rows, tile), F32)
            for d in range(4):
                acc += jnp.dot(
                    GT[d], H[d, :, :, where].reshape(2 * tl, tile), preferred_element_type=F32
                )
            HO[:, where] = acc.astype(BF16)
            head_copy(t).start()
            return carry

        lax.fori_loop(low, high, body, 0)

    gradient(3, 0)
    gradient(1, 0)
    send_first(0, 0, (0,))
    send_first(0, 1, (0,))
    gradient(3, 1)
    gradient(2, 1)
    send_first(0, 0, (1,))
    send_first(0, 1, (1,))
    for d, s in ((2, 0), (1, 1), (0, 0), (0, 1)):
        gradient(d, s)
    send_first(1, 0)
    head(0, 1)
    send_second(0, 0)
    send_first(1, 1)
    head(1, 2)
    send_second(0, 1)
    send_first(2, 0)
    head(2, 3)
    send_second(1, 0)
    send_vocab(0, 0)
    send_first(2, 1)
    head(3, 4)
    send_second(1, 1)
    send_vocab(0, 1)
    send_first(3, 0)
    head(4, 5)
    send_second(2, 0)
    send_vocab(1, 0)
    send_first(3, 1)
    head(5, 6)
    send_second(2, 1)
    send_vocab(1, 1)
    head(6, 7)
    send_second(3, 0)
    send_vocab(2, 0)
    head(7, head_tiles)
    send_second(3, 1)
    send_vocab(2, 1)
    send_vocab(3, 0)
    send_vocab(3, 1)
    own = pl.ds(0, cw) if m == 1 else pl.ds(pl.multiple_of(zm * cw, cw), cw)
    for cp in cz:
        cp.wait_recv()
    for s in range(2):
        total = FA[s, :, own]
        for x in range(1, n):
            total = total + ZR[x, s].astype(F32)
        GO[s] = total.astype(BF16)
    out = pltpu.make_async_copy(GO, gh_out, lsem.at[2])
    out.start()
    to_partner.wait_send()
    for cp in ag:
        cp.wait_send()
    for j in range(3):
        for d in (1, 2, 3):
            chain_wait_send(j, d)
    for cp in list(c1.values()) + list(c2.values()) + cz:
        cp.wait_send()

    def drain(t, carry):
        head_copy(t).wait()
        return carry

    lax.fori_loop(0, head_tiles, drain, 0)
    out.wait()


def hand_over(hid_ref, head_ref, hid_out, head_out, sems):
    rows = head_ref.shape[0]
    count = 8
    step = rows // count
    copies = [pltpu.make_async_copy(hid_ref, hid_out, sems.at[count])]
    for t in range(count):
        part = pl.ds(t * step, step)
        copies.append(pltpu.make_async_copy(head_ref.at[part], head_out.at[part], sems.at[t]))
    for cp in copies:
        cp.start()
    for cp in copies:
        cp.wait()


def solution(mesh):
    n = mesh.shape["vocab"]

    def local(hidden, head_weight, labels, token_mask, other_logps, ref_logps):
        tl = hidden.shape[1]
        rows, half = head_weight.shape
        toks = labels.shape[1]
        CW, cw = half // PARTS, half // n
        vm = pltpu.VMEM
        dma = pltpu.SemaphoreType.DMA
        any_spec = pl.BlockSpec(memory_space=pl.ANY)
        vmem_spec = pl.BlockSpec(memory_space=pltpu.VMEM)
        results = pl.pallas_call(
            functools.partial(kernel, n),
            out_shape=(
                jax.ShapeDtypeStruct((2, tl, cw), BF16),
                jax.ShapeDtypeStruct((rows, half), BF16),
            ),
            in_specs=[any_spec, any_spec] + [vmem_spec] * 4,
            out_specs=(any_spec, any_spec),
            scratch_shapes=[
                vm((rows, half), BF16),
                vm((4, 2, tl, half), BF16),
                vm((4, rows, 2 * tl), F32),
                vm((4, rows, 2 * tl), F32),
                vm((4, rows, 2 * tl), BF16),
                vm((4, 2, tl, rows), BF16),
                vm((PARTS, 2, 2, tl, CW), BF16),
                vm((PARTS, 2, 2, tl, CW), BF16),
                vm((PARTS, 2, tl, CW), BF16),
                vm((PARTS, 2, tl, CW), BF16),
                vm((PARTS, 2, tl, CW), BF16),
                vm((n, 2, tl, cw), BF16),
                vm((2, tl, CW), F32),
                vm((rows, half), BF16),
                vm((2, tl, cw), BF16),
                vm((3, 8, tl), F32),
                vm((3, 8, tl), F32),
                vm((n, 3, 8, tl), F32),
                vm((4, 3, 8, tl), F32),
                vm((2, 8, tl), F32),
                vm((2, 8, toks), jnp.int32),
                vm((2, 8, 128), F32),
                dma((3,)),
                dma((2,)),
                dma((4,)),
                dma((4, 2)),
                dma((4, 2)),
                dma((4, 2, 2)),
                dma((4, 2, 2)),
                dma((2, 3, 4)),
                dma((2, 3, 4)),
                dma((4,)),
                dma((4,)),
                dma((n,)),
                dma((n,)),
                dma((4,)),
                dma((4,)),
                dma((PARTS, 2, 2)),
                dma((PARTS, 2, 2)),
                dma((PARTS, 2, 2)),
                dma((PARTS, 2, 2)),
                dma((n, 2)),
                dma((n, 2)),
                dma((half // 512,)),
            ],
            compiler_params=pltpu.CompilerParams(
                collective_id=0, has_side_effects=True, vmem_limit_bytes=58 * 1024 * 1024
            ),
            cost_estimate=pl.CostEstimate(
                flops=6 * 8 * tl * rows * half, bytes_accessed=6 * rows * half, transcendentals=0
            ),
        )(
            hidden, head_weight, labels, token_mask,
            other_logps.reshape(1, 1), ref_logps.reshape(1, 1),
        )
        return pl.pallas_call(
            hand_over,
            out_shape=tuple(jax.ShapeDtypeStruct(r.shape, r.dtype) for r in results),
            in_specs=[any_spec, any_spec],
            out_specs=(any_spec, any_spec),
            scratch_shapes=[dma((9,))],
            cost_estimate=pl.CostEstimate(
                flops=0, bytes_accessed=4 * rows * half, transcendentals=0
            ),
        )(*results)

    return jax.shard_map(
        local,
        mesh=mesh,
        in_specs=(
            P("pair", "ctx", None),
            P(("ctx", "vocab"), "pair"),
            P("pair", None),
            P("pair", None),
            P("pair"),
            P("pair"),
        ),
        out_specs=(P(None, "ctx", ("pair", "vocab")), P(("ctx", "vocab"), "pair")),
        check_vma=False,
    )
```

```python
import functools

import jax
import jax.numpy as jnp
from jax import lax
from jax.experimental import pallas as pl
from jax.experimental.pallas import tpu as pltpu
from jax.sharding import PartitionSpec as P

beta_value = 0.01
z_weight = 0.0001
loss_scale = 4096.0
F32, BF16 = jnp.float32, jnp.bfloat16
PARTS = 4


def flip(index, mask):
    bit = 1
    while bit <= mask:
        if mask & bit:
            index = index + bit * (1 - 2 * lax.rem(lax.div(index, bit), 2))
        bit *= 2
    return index


def kernel(
    n, hid, w_hbm, lab_in, msk_in, oth_in, ref_in, gh_out, head_out,
    w, HX, H, LT, LR, GT, G, S1, R1, S2, R2, ZS, ZR, FA, HO, GO, st, st2, zst, cst, ab, auxi, auxf,
    lsem, psem, aux_sem, az_s, az_r, ag_s, ag_r, ch_s, ch_r, lt_s, lt_r, zst_s, zst_r, cst_s, cst_r,
    s1_s, s1_r, s2_s, s2_r, z_s, z_r, ho_sem,
):
    p, c, z = lax.axis_index("pair"), lax.axis_index("ctx"), lax.axis_index("vocab")
    q = 1 - p
    partner = (q, c, z)
    tl = H.shape[2]
    half = w.shape[1]
    rows = w.shape[0]
    m = n // PARTS
    cw = half // n
    CW = half // PARTS
    ktile = 512
    zs = lax.div(z, m)
    zq = half * 3 // (8 * PARTS)
    rest = slice(zq * PARTS, half)
    hr = tl // 2

    def at_ctx(d):
        return (p, flip(c, d), z)

    def at_vocab(x):
        return (p, c, flip(z, x))

    def remote(src, dst, ss, rs, dev):
        return pltpu.make_async_remote_copy(
            src_ref=src, dst_ref=dst, send_sem=ss, recv_sem=rs,
            device_id=dev, device_id_type=pl.DeviceIdType.MESH,
        )

    own_cols = pl.ds(pl.multiple_of(p * half, half), half)
    other_cols = pl.ds(pl.multiple_of(q * half, half), half)
    cp_h = pltpu.make_async_copy(hid.at[0, :, own_cols], H.at[0, p], lsem.at[1])
    cp_x = pltpu.make_async_copy(hid.at[0, :, other_cols], HX, lsem.at[3])
    cp_x.start()
    cp_h.start()
    cp_w = pltpu.make_async_copy(w_hbm, w, lsem.at[0])
    cp_w.start()
    auxi[p, 0:1, :] = lab_in[...]
    auxi[p, 1:2, :] = msk_in[...]
    auxf[p, 0:1, :] = jnp.broadcast_to(oth_in[...], (1, 128))
    auxf[p, 1:2, :] = jnp.broadcast_to(ref_in[...], (1, 128))

    barrier = pltpu.get_barrier_semaphore()
    peers = [partner] + [at_ctx(d) for d in (1, 2, 3)] + [at_vocab(x) for x in range(1, n)]
    for dev in peers:
        pl.semaphore_signal(barrier, inc=1, device_id=dev, device_id_type=pl.DeviceIdType.MESH)
    pl.semaphore_wait(barrier, len(peers))

    cp_x.wait()
    to_partner = remote(HX, H.at[0, p], psem.at[0], psem.at[1], partner)
    to_partner.start()
    cp_h.wait()
    ag = []

    def zcols(k):
        return pl.ds(pl.multiple_of(k * zq, zq), zq)

    def send_z(d, s, src, to, into):
        cp = remote(src, H.at[into, s, :, zcols(zs)], az_s.at[into, s], az_r.at[into, s], at_ctx(to))
        cp.start()
        ag.append(cp)

    def send_rest(h, s, src, to, into):
        cp = remote(
            src, H.at[into, s, h * hr : (h + 1) * hr, rest],
            ag_s.at[into, s, h], ag_r.at[into, s, h], at_ctx(to),
        )
        cp.start()
        ag.append(cp)

    def held_rest(d, s, h):
        return H.at[d, s, h * hr : (h + 1) * hr, rest]

    own_z = H.at[0, p, :, zcols(zs)]
    for d in (1, 2):
        send_z(0, p, own_z, d, d)
    for d in (1, 2):
        send_rest(0, p, held_rest(0, p, 0), d, d)
    ax = [
        remote(auxi.at[p], auxi.at[p], aux_sem.at[0], aux_sem.at[1], partner),
        remote(auxf.at[p], auxf.at[p], aux_sem.at[2], aux_sem.at[3], partner),
    ]
    for cp in ax:
        cp.start()
    to_partner.wait_recv()
    for d in (1, 2):
        send_z(0, q, H.at[0, q, :, zcols(zs)], d, d)
    for d in (1, 2):
        send_rest(1, p, held_rest(0, p, 1), d, d)

    def z_wait(d, s):
        part = H.at[d, s, :, zcols(zs)]
        remote(part, part, az_s.at[d, s], az_r.at[d, s], at_ctx(d)).wait_recv()

    def rest_wait(d, s):
        for h in range(2):
            part = held_rest(d, s, h)
            remote(part, part, ag_s.at[d, s, h], ag_r.at[d, s, h], at_ctx(d)).wait_recv()

    def chain_copy(way, j, d, part):
        piece = H.at[d, :, :, zcols(part)]
        dev = (p, c, lax.rem(z + n + (m if way == 0 else -m), n))
        return remote(piece, piece, ch_s.at[way, j, d], ch_r.at[way, j, d], dev)

    def chain_sent(way, j):
        part = zs - j if way == 0 else zs + j
        if way == 0:
            return part, jnp.logical_and(zs < PARTS - 1, part >= 0)
        return part, jnp.logical_and(zs > 0, part < PARTS)

    def chain_send(j, blocks):
        for d in blocks:
            for way in range(2):
                part, there = chain_sent(way, j)

                @pl.when(there)
                def _():
                    chain_copy(way, j, d, part).start()

    def chain_wait_send(j, d):
        for way in range(2):
            part, there = chain_sent(way, j)

            @pl.when(there)
            def _():
                chain_copy(way, j, d, part).wait_send()

    def chain_recv(j, blocks):
        for d in blocks:
            for way in range(2):
                part = zs - 1 - j if way == 0 else zs + 1 + j

                @pl.when(part >= 0 if way == 0 else part < PARTS)
                def _():
                    chain_copy(way, j, d, part).wait_recv()

    z_wait(1, 0)
    send_z(1, 0, H.at[1, 0, :, zcols(zs)], 2, 3)
    z_wait(2, 1)
    send_z(2, 1, H.at[2, 1, :, zcols(zs)], 1, 3)
    for h in range(2):
        for d in (1, 2):
            send_rest(h, q, held_rest(0, q, h), d, d)
    z_wait(1, 1)
    z_wait(2, 0)
    chain_send(0, (1, 2))
    cp_w.wait()

    lt_copies = []

    def add_logits(d, low, high):
        def body(k, carry):
            cols = pl.ds(pl.multiple_of(k * ktile, ktile), ktile)
            block = H[d, :, :, cols].reshape(2 * tl, ktile)
            LT[d] += lax.dot_general(
                w[:, cols], block, (((1,), (1,)), ((), ())), preferred_element_type=F32
            )
            return carry

        lax.fori_loop(low // ktile, high // ktile, body, 0)

    def swap_logits(d):
        cp = remote(LT.at[d], LR.at[d], lt_s.at[d], lt_r.at[d], partner)
        cp.start()
        lt_copies.append(cp)

    chained = zq * PARTS

    base = (c * n + z) * rows

    def is_label(d, s):
        toks = pl.ds(pl.multiple_of(flip(c, d) * tl, tl), tl)
        return lax.broadcasted_iota(jnp.int32, (rows, tl), 0) == auxi[s, 0:1, toks] - base

    def local_stats(d):
        lt_copies[d].wait()
        for s in range(2):
            u = 2 * d + s
            lanes = slice(s * tl, (s + 1) * tl)
            l = LT[d, :, lanes] + LR[d, :, lanes]
            top = jnp.max(l, axis=0, keepdims=True)
            e = jnp.exp(l - top)
            LT[d, :, lanes] = e
            st[0, u : u + 1, :] = top
            st[1, u : u + 1, :] = jnp.sum(e, axis=0, keepdims=True)
            st[2, u : u + 1, :] = jnp.sum(
                jnp.where(is_label(d, s), l, 0.0), axis=0, keepdims=True
            )

    for d in range(4):
        LT[d] = jnp.zeros((rows, 2 * tl), F32)
    add_logits(0, 0, half)
    swap_logits(0)
    z_wait(3, 0)
    z_wait(3, 1)
    chain_send(0, (3,))
    chain_recv(0, (1, 2))
    chain_send(1, (1, 2))
    chain_recv(0, (3,))
    chain_send(1, (3,))
    for cp in ax:
        cp.wait()
    local_stats(0)
    chain_recv(1, (1, 2))
    chain_send(2, (1, 2))
    rest_wait(1, 0)
    for h in range(2):
        send_rest(h, 0, held_rest(1, 0, h), 2, 3)
    rest_wait(2, 1)
    for h in range(2):
        send_rest(h, 1, held_rest(2, 1, h), 1, 3)
    chain_recv(1, (3,))
    chain_send(2, (3,))
    rest_wait(1, 1)
    rest_wait(2, 0)
    add_logits(1, chained, half)
    add_logits(2, chained, half)
    chain_recv(2, (1, 2))
    add_logits(1, 0, chained)
    swap_logits(1)
    add_logits(2, 0, chained)
    swap_logits(2)
    local_stats(1)
    chain_recv(2, (3,))
    add_logits(3, 0, chained)
    rest_wait(3, 0)
    rest_wait(3, 1)
    add_logits(3, chained, half)
    swap_logits(3)
    local_stats(2)
    local_stats(3)

    zc = []
    for x in range(1, n):
        cp = remote(st, zst.at[x], zst_s.at[x], zst_r.at[x], at_vocab(x))
        cp.start()
        zc.append(cp)
    for cp in zc:
        cp.wait()

    def merge(parts):
        top = functools.reduce(jnp.maximum, [t for t, _, _ in parts])
        total = sum(s * jnp.exp(t - top) for t, s, _ in parts)
        label = sum(l for _, _, l in parts)
        return top, total, label

    def read(ref, *at):
        return tuple(ref[(*at, r)] for r in range(3))

    got = merge([read(st)] + [read(zst, x) for x in range(1, n)])
    for r in range(3):
        st2[r] = got[r]
    cc = []
    for k in (3, 1, 2):
        cp = remote(st2, cst.at[k], cst_s.at[k], cst_r.at[k], at_ctx(k))
        cp.start()
        cc.append(cp)
    for cp in cc:
        cp.wait()

    def read_ctx(k):
        return tuple(
            jnp.concatenate(
                [cst[k, r, 2 * (k ^ d) : 2 * (k ^ d) + 2, :] for d in range(4)], axis=0
            )
            for r in range(3)
        )

    top, total, label = merge([got] + [read_ctx(k) for k in (1, 2, 3)])
    lt = top + jnp.log(total)
    mask_rows = []
    for d in range(4):
        toks = pl.ds(pl.multiple_of(flip(c, d) * tl, tl), tl)
        mask_rows += [auxi[0, 1:2, toks], auxi[1, 1:2, toks]]
    mk = jnp.concatenate(mask_rows, axis=0).astype(F32)
    response = lax.rem(lax.broadcasted_iota(jnp.int32, (8, tl), 0), 2)
    counted = mk * (label - lt)
    relative = []
    for s in range(2):
        part = jnp.sum(jnp.where(response == s, counted, 0.0), axis=0, keepdims=True)
        slice_sum = jnp.sum(part, axis=1, keepdims=True)
        relative.append((slice_sum + auxf[s, 0:1, 0:1]) - auxf[s, 1:2, 0:1])
    margin = beta_value * (relative[0] - relative[1])
    coef = beta_value / (1.0 + jnp.exp(margin))
    seq = jnp.where(response == 1, coef, -coef)
    ab[0] = loss_scale * mk * (2.0 * z_weight * lt - seq) * jnp.exp(st[0] - lt)
    ab[1] = loss_scale * mk * seq

    def gradient(d, s):
        u = 2 * d + s
        lanes = slice(s * tl, (s + 1) * tl)
        b = jnp.where(is_label(d, s), ab[1, u : u + 1, :], 0.0)
        g = LT[d, :, lanes] * ab[0, u : u + 1, :] + b
        GT[d, :, lanes] = g.astype(BF16)
        G[d, s] = g.T.astype(BF16)

    first, second = (1, 2), (2, 1)

    def cols(i):
        return pl.ds(pl.multiple_of(flip(zs, PARTS - 1 - i) * CW, CW), CW)

    def term(d, s, i):
        return jnp.dot(G[d, s], w[:, cols(i)], preferred_element_type=F32)

    c1, c2, cz = {}, {}, []
    second_term, own_term = {}, {}

    def send_first(i, h, responses=(0, 1)):
        hs = slice(h * hr, (h + 1) * hr)
        for s in responses:
            f = first[s]
            if h == 0:
                S1[i, s, 1] = term(3, s, i).astype(BF16)
                S1[i, s, 0] = term(f, s, i).astype(BF16)
            cp = remote(
                S1.at[i, s, :, hs], R1.at[i, s, :, hs],
                s1_s.at[i, s, h], s1_r.at[i, s, h], at_ctx(f),
            )
            cp.start()
            c1[i, s, h] = cp

    def send_second(i, h):
        hs = slice(h * hr, (h + 1) * hr)
        for s in range(2):
            g = second[s]
            if h == 0:
                second_term[s] = term(g, s, i)
            c1[i, s, h].wait_recv()
            S2[i, s, hs] = (second_term[s][hs] + R1[i, s, 1, hs].astype(F32)).astype(BF16)
            cp = remote(
                S2.at[i, s, hs], R2.at[i, s, hs], s2_s.at[i, s, h], s2_r.at[i, s, h], at_ctx(g)
            )
            cp.start()
            c2[i, s, h] = cp

    zm = lax.rem(z, m)

    def send_vocab(i, h):
        hs = slice(h * hr, (h + 1) * hr)
        for s in range(2):
            if h == 0:
                own_term[s] = term(0, s, i)
            mine = own_term[s][hs] + R1[i, s, 0, hs].astype(F32)
            c2[i, s, h].wait_recv()
            mine = mine + R2[i, s, hs].astype(F32)
            if i == PARTS - 1:
                FA[s, hs] = mine
            ZS[i, s, hs] = mine.astype(BF16)
        for k in reversed(range(m)):
            x = (PARTS - 1 - i) * m + k
            if x == 0:
                continue
            if m == 1:
                src = ZS.at[i, :, hs]
            else:
                src = ZS.at[i, :, hs, pl.ds(pl.multiple_of(flip(zm, k) * cw, cw), cw)]
            cp = remote(src, ZR.at[x, :, hs], z_s.at[x, h], z_r.at[x, h], at_vocab(x))
            cp.start()
            cz.append(cp)

    tile = 512
    head_tiles = half // tile

    def head_copy(t):
        where = pl.ds(pl.multiple_of(t * tile, tile), tile)
        return pltpu.make_async_copy(HO.at[:, where], head_out.at[:, where], ho_sem.at[t])

    def head(low, high):
        def body(t, carry):
            where = pl.ds(pl.multiple_of(t * tile, tile), tile)
            acc = jnp.zeros((rows, tile), F32)
            for d in range(4):
                acc += jnp.dot(
                    GT[d], H[d, :, :, where].reshape(2 * tl, tile), preferred_element_type=F32
                )
            HO[:, where] = acc.astype(BF16)
            head_copy(t).start()
            return carry

        lax.fori_loop(low, high, body, 0)

    gradient(3, 0)
    gradient(1, 0)
    send_first(0, 0, (0,))
    send_first(0, 1, (0,))
    gradient(3, 1)
    gradient(2, 1)
    send_first(0, 0, (1,))
    send_first(0, 1, (1,))
    for d, s in ((2, 0), (1, 1), (0, 0), (0, 1)):
        gradient(d, s)
    send_first(1, 0)
    head(0, 1)
    send_second(0, 0)
    send_first(1, 1)
    head(1, 2)
    send_second(0, 1)
    send_first(2, 0)
    head(2, 3)
    send_second(1, 0)
    send_vocab(0, 0)
    send_first(2, 1)
    head(3, 4)
    send_second(1, 1)
    send_vocab(0, 1)
    send_first(3, 0)
    head(4, 5)
    send_second(2, 0)
    send_vocab(1, 0)
    send_first(3, 1)
    head(5, 6)
    send_second(2, 1)
    send_vocab(1, 1)
    head(6, 7)
    send_second(3, 0)
    send_vocab(2, 0)
    head(7, head_tiles)
    send_second(3, 1)
    send_vocab(2, 1)
    send_vocab(3, 0)
    send_vocab(3, 1)
    own = pl.ds(0, cw) if m == 1 else pl.ds(pl.multiple_of(zm * cw, cw), cw)
    for cp in cz:
        cp.wait_recv()
    for s in range(2):
        total = FA[s, :, own]
        for x in range(1, n):
            total = total + ZR[x, s].astype(F32)
        GO[s] = total.astype(BF16)
    out = pltpu.make_async_copy(GO, gh_out, lsem.at[2])
    out.start()
    to_partner.wait_send()
    for cp in ag:
        cp.wait_send()
    for j in range(3):
        for d in (1, 2, 3):
            chain_wait_send(j, d)
    for cp in list(c1.values()) + list(c2.values()) + cz:
        cp.wait_send()

    def drain(t, carry):
        head_copy(t).wait()
        return carry

    lax.fori_loop(0, head_tiles, drain, 0)
    out.wait()


def hand_over(hid_ref, head_ref, hid_out, head_out, hid_v, head_v, in_sems, out_sems):
    rows = head_ref.shape[0]
    count = 8
    step = rows // count
    pieces = [(hid_ref, hid_v, hid_out)]
    for t in range(count):
        part = pl.ds(t * step, step)
        pieces.append((head_ref.at[part], head_v.at[part], head_out.at[part]))
    reads = [pltpu.make_async_copy(a, v, in_sems.at[t]) for t, (a, v, _) in enumerate(pieces)]
    writes = [pltpu.make_async_copy(v, o, out_sems.at[t]) for t, (_, v, o) in enumerate(pieces)]
    for cp in reads:
        cp.start()
    for cp, out in zip(reads, writes):
        cp.wait()
        out.start()
    for cp in writes:
        cp.wait()


def solution(mesh):
    n = mesh.shape["vocab"]

    def local(hidden, head_weight, labels, token_mask, other_logps, ref_logps):
        tl = hidden.shape[1]
        rows, half = head_weight.shape
        toks = labels.shape[1]
        CW, cw = half // PARTS, half // n
        vm = pltpu.VMEM
        dma = pltpu.SemaphoreType.DMA
        any_spec = pl.BlockSpec(memory_space=pl.ANY)
        vmem_spec = pl.BlockSpec(memory_space=pltpu.VMEM)
        results = pl.pallas_call(
            functools.partial(kernel, n),
            out_shape=(
                jax.ShapeDtypeStruct((2, tl, cw), BF16),
                jax.ShapeDtypeStruct((rows, half), BF16),
            ),
            in_specs=[any_spec, any_spec] + [vmem_spec] * 4,
            out_specs=(any_spec, any_spec),
            scratch_shapes=[
                vm((rows, half), BF16),
                vm((tl, half), BF16),
                vm((4, 2, tl, half), BF16),
                vm((4, rows, 2 * tl), F32),
                vm((4, rows, 2 * tl), F32),
                vm((4, rows, 2 * tl), BF16),
                vm((4, 2, tl, rows), BF16),
                vm((PARTS, 2, 2, tl, CW), BF16),
                vm((PARTS, 2, 2, tl, CW), BF16),
                vm((PARTS, 2, tl, CW), BF16),
                vm((PARTS, 2, tl, CW), BF16),
                vm((PARTS, 2, tl, CW), BF16),
                vm((n, 2, tl, cw), BF16),
                vm((2, tl, CW), F32),
                vm((rows, half), BF16),
                vm((2, tl, cw), BF16),
                vm((3, 8, tl), F32),
                vm((3, 8, tl), F32),
                vm((n, 3, 8, tl), F32),
                vm((4, 3, 8, tl), F32),
                vm((2, 8, tl), F32),
                vm((2, 8, toks), jnp.int32),
                vm((2, 8, 128), F32),
                dma((4,)),
                dma((2,)),
                dma((4,)),
                dma((4, 2)),
                dma((4, 2)),
                dma((4, 2, 2)),
                dma((4, 2, 2)),
                dma((2, 3, 4)),
                dma((2, 3, 4)),
                dma((4,)),
                dma((4,)),
                dma((n,)),
                dma((n,)),
                dma((4,)),
                dma((4,)),
                dma((PARTS, 2, 2)),
                dma((PARTS, 2, 2)),
                dma((PARTS, 2, 2)),
                dma((PARTS, 2, 2)),
                dma((n, 2)),
                dma((n, 2)),
                dma((half // 512,)),
            ],
            compiler_params=pltpu.CompilerParams(
                collective_id=0, has_side_effects=True, vmem_limit_bytes=58 * 1024 * 1024
            ),
            cost_estimate=pl.CostEstimate(
                flops=6 * 8 * tl * rows * half, bytes_accessed=6 * rows * half, transcendentals=0
            ),
        )(
            hidden, head_weight, labels, token_mask,
            other_logps.reshape(1, 1), ref_logps.reshape(1, 1),
        )
        return pl.pallas_call(
            hand_over,
            out_shape=tuple(jax.ShapeDtypeStruct(r.shape, r.dtype) for r in results),
            in_specs=[any_spec, any_spec],
            out_specs=(any_spec, any_spec),
            scratch_shapes=[vm(r.shape, r.dtype) for r in results] + [dma((9,)), dma((9,))],
            compiler_params=pltpu.CompilerParams(vmem_limit_bytes=24 * 1024 * 1024),
            cost_estimate=pl.CostEstimate(
                flops=0, bytes_accessed=4 * rows * half, transcendentals=0
            ),
        )(*results)

    return jax.shard_map(
        local,
        mesh=mesh,
        in_specs=(
            P("pair", "ctx", None),
            P(("ctx", "vocab"), "pair"),
            P("pair", None),
            P("pair", None),
            P("pair"),
            P("pair"),
        ),
        out_specs=(P(None, "ctx", ("pair", "vocab")), P(("ctx", "vocab"), "pair")),
        check_vma=False,
    )
```

```python
import functools

import jax
import jax.numpy as jnp
from jax import lax
from jax.experimental import pallas as pl
from jax.experimental.pallas import tpu as pltpu
from jax.sharding import PartitionSpec as P

beta_value = 0.01
z_weight = 0.0001
loss_scale = 4096.0
F32, BF16 = jnp.float32, jnp.bfloat16
PARTS = 4


def flip(index, mask):
    bit = 1
    while bit <= mask:
        if mask & bit:
            index = index + bit * (1 - 2 * lax.rem(lax.div(index, bit), 2))
        bit *= 2
    return index


def kernel(
    n, hid, w_hbm, lab_in, msk_in, oth_in, ref_in, gh_out, head_out,
    w, HX, H, LT, LR, GT, G, S1, R1, S2, R2, ZS, ZR, FA, HO, GO, st, st2, zst, cst, ab, auxi, auxf,
    lsem, psem, aux_sem, az_s, az_r, ag_s, ag_r, ch_s, ch_r, lt_s, lt_r, zst_s, zst_r, cst_s, cst_r,
    s1_s, s1_r, s2_s, s2_r, z_s, z_r, ho_sem,
):
    p, c, z = lax.axis_index("pair"), lax.axis_index("ctx"), lax.axis_index("vocab")
    q = 1 - p
    partner = (q, c, z)
    tl = H.shape[2]
    half = w.shape[1]
    rows = w.shape[0]
    m = n // PARTS
    cw = half // n
    CW = half // PARTS
    ktile = 512
    zs = lax.div(z, m)
    zq = half * 3 // (8 * PARTS)
    rest = slice(zq * PARTS, half)
    hr = tl // 2

    def at_ctx(d):
        return (p, flip(c, d), z)

    def at_vocab(x):
        return (p, c, flip(z, x))

    def remote(src, dst, ss, rs, dev):
        return pltpu.make_async_remote_copy(
            src_ref=src, dst_ref=dst, send_sem=ss, recv_sem=rs,
            device_id=dev, device_id_type=pl.DeviceIdType.MESH,
        )

    own_cols = pl.ds(pl.multiple_of(p * half, half), half)
    other_cols = pl.ds(pl.multiple_of(q * half, half), half)
    cp_h = pltpu.make_async_copy(hid.at[0, :, own_cols], H.at[0, p], lsem.at[1])
    cp_x = pltpu.make_async_copy(hid.at[0, :, other_cols], HX, lsem.at[3])
    cp_x.start()
    cp_h.start()
    cp_w = pltpu.make_async_copy(w_hbm, w, lsem.at[0])
    cp_w.start()
    auxi[p, 0:1, :] = lab_in[...]
    auxi[p, 1:2, :] = msk_in[...]
    auxf[p, 0:1, :] = jnp.broadcast_to(oth_in[...], (1, 128))
    auxf[p, 1:2, :] = jnp.broadcast_to(ref_in[...], (1, 128))

    barrier = pltpu.get_barrier_semaphore()
    peers = [partner] + [at_ctx(d) for d in (1, 2, 3)] + [at_vocab(x) for x in range(1, n)]
    for dev in peers:
        pl.semaphore_signal(barrier, inc=1, device_id=dev, device_id_type=pl.DeviceIdType.MESH)
    pl.semaphore_wait(barrier, len(peers))

    cp_x.wait()
    to_partner = remote(HX, H.at[0, p], psem.at[0], psem.at[1], partner)
    to_partner.start()
    cp_h.wait()
    ag = []

    def zcols(k):
        return pl.ds(pl.multiple_of(k * zq, zq), zq)

    def send_z(d, s, src, to, into):
        cp = remote(src, H.at[into, s, :, zcols(zs)], az_s.at[into, s], az_r.at[into, s], at_ctx(to))
        cp.start()
        ag.append(cp)

    def send_rest(h, s, src, to, into):
        cp = remote(
            src, H.at[into, s, h * hr : (h + 1) * hr, rest],
            ag_s.at[into, s, h], ag_r.at[into, s, h], at_ctx(to),
        )
        cp.start()
        ag.append(cp)

    def held_rest(d, s, h):
        return H.at[d, s, h * hr : (h + 1) * hr, rest]

    own_z = H.at[0, p, :, zcols(zs)]
    for d in (1, 2):
        send_z(0, p, own_z, d, d)
    for d in (1, 2):
        send_rest(0, p, held_rest(0, p, 0), d, d)
    ax = [
        remote(auxi.at[p], auxi.at[p], aux_sem.at[0], aux_sem.at[1], partner),
        remote(auxf.at[p], auxf.at[p], aux_sem.at[2], aux_sem.at[3], partner),
    ]
    for cp in ax:
        cp.start()
    to_partner.wait_recv()
    for d in (1, 2):
        send_z(0, q, H.at[0, q, :, zcols(zs)], d, d)
    for d in (1, 2):
        send_rest(1, p, held_rest(0, p, 1), d, d)

    def z_wait(d, s):
        part = H.at[d, s, :, zcols(zs)]
        remote(part, part, az_s.at[d, s], az_r.at[d, s], at_ctx(d)).wait_recv()

    def rest_wait(d, s):
        for h in range(2):
            part = held_rest(d, s, h)
            remote(part, part, ag_s.at[d, s, h], ag_r.at[d, s, h], at_ctx(d)).wait_recv()

    def chain_copy(way, j, d, part):
        piece = H.at[d, :, :, zcols(part)]
        dev = (p, c, lax.rem(z + n + (m if way == 0 else -m), n))
        return remote(piece, piece, ch_s.at[way, j, d], ch_r.at[way, j, d], dev)

    def chain_sent(way, j):
        part = zs - j if way == 0 else zs + j
        if way == 0:
            return part, jnp.logical_and(zs < PARTS - 1, part >= 0)
        return part, jnp.logical_and(zs > 0, part < PARTS)

    def chain_send(j, blocks):
        for d in blocks:
            for way in range(2):
                part, there = chain_sent(way, j)

                @pl.when(there)
                def _():
                    chain_copy(way, j, d, part).start()

    def chain_wait_send(j, d):
        for way in range(2):
            part, there = chain_sent(way, j)

            @pl.when(there)
            def _():
                chain_copy(way, j, d, part).wait_send()

    def chain_recv(j, blocks):
        for d in blocks:
            for way in range(2):
                part = zs - 1 - j if way == 0 else zs + 1 + j

                @pl.when(part >= 0 if way == 0 else part < PARTS)
                def _():
                    chain_copy(way, j, d, part).wait_recv()

    z_wait(1, 0)
    send_z(1, 0, H.at[1, 0, :, zcols(zs)], 2, 3)
    z_wait(2, 1)
    send_z(2, 1, H.at[2, 1, :, zcols(zs)], 1, 3)
    for h in range(2):
        for d in (1, 2):
            send_rest(h, q, held_rest(0, q, h), d, d)
    z_wait(1, 1)
    z_wait(2, 0)
    chain_send(0, (1, 2))
    cp_w.wait()

    lt_copies = []

    def add_logits(d, low, high):
        def body(k, carry):
            cols = pl.ds(pl.multiple_of(k * ktile, ktile), ktile)
            block = H[d, :, :, cols].reshape(2 * tl, ktile)
            LT[d] += lax.dot_general(
                w[:, cols], block, (((1,), (1,)), ((), ())), preferred_element_type=F32
            )
            return carry

        lax.fori_loop(low // ktile, high // ktile, body, 0)

    def swap_logits(d):
        cp = remote(LT.at[d], LR.at[d], lt_s.at[d], lt_r.at[d], partner)
        cp.start()
        lt_copies.append(cp)

    chained = zq * PARTS

    base = (c * n + z) * rows

    def is_label(d, s):
        toks = pl.ds(pl.multiple_of(flip(c, d) * tl, tl), tl)
        return lax.broadcasted_iota(jnp.int32, (rows, tl), 0) == auxi[s, 0:1, toks] - base

    def local_stats(d):
        lt_copies[d].wait()
        for s in range(2):
            u = 2 * d + s
            lanes = slice(s * tl, (s + 1) * tl)
            l = LT[d, :, lanes] + LR[d, :, lanes]
            top = jnp.max(l, axis=0, keepdims=True)
            e = jnp.exp(l - top)
            LT[d, :, lanes] = e
            st[0, u : u + 1, :] = top
            st[1, u : u + 1, :] = jnp.sum(e, axis=0, keepdims=True)
            st[2, u : u + 1, :] = jnp.sum(
                jnp.where(is_label(d, s), l, 0.0), axis=0, keepdims=True
            )

    for d in range(4):
        LT[d] = jnp.zeros((rows, 2 * tl), F32)
    add_logits(0, 0, half)
    swap_logits(0)
    z_wait(3, 0)
    z_wait(3, 1)
    chain_send(0, (3,))
    chain_recv(0, (1, 2))
    chain_send(1, (1, 2))
    chain_recv(0, (3,))
    chain_send(1, (3,))
    for cp in ax:
        cp.wait()
    local_stats(0)
    chain_recv(1, (1, 2))
    chain_send(2, (1, 2))
    rest_wait(1, 0)
    for h in range(2):
        send_rest(h, 0, held_rest(1, 0, h), 2, 3)
    rest_wait(2, 1)
    for h in range(2):
        send_rest(h, 1, held_rest(2, 1, h), 1, 3)
    chain_recv(1, (3,))
    chain_send(2, (3,))
    rest_wait(1, 1)
    rest_wait(2, 0)
    add_logits(1, chained, half)
    add_logits(2, chained, half)
    chain_recv(2, (1, 2))
    add_logits(1, 0, chained)
    swap_logits(1)
    add_logits(2, 0, chained)
    swap_logits(2)
    local_stats(1)
    chain_recv(2, (3,))
    add_logits(3, 0, chained)
    rest_wait(3, 0)
    rest_wait(3, 1)
    add_logits(3, chained, half)
    swap_logits(3)
    local_stats(2)
    local_stats(3)

    zc = []
    for x in range(1, n):
        cp = remote(st, zst.at[x], zst_s.at[x], zst_r.at[x], at_vocab(x))
        cp.start()
        zc.append(cp)
    for cp in zc:
        cp.wait()

    def merge(parts):
        top = functools.reduce(jnp.maximum, [t for t, _, _ in parts])
        total = sum(s * jnp.exp(t - top) for t, s, _ in parts)
        label = sum(l for _, _, l in parts)
        return top, total, label

    def read(ref, *at):
        return tuple(ref[(*at, r)] for r in range(3))

    got = merge([read(st)] + [read(zst, x) for x in range(1, n)])
    for r in range(3):
        st2[r] = got[r]
    cc = []
    for k in (3, 1, 2):
        cp = remote(st2, cst.at[k], cst_s.at[k], cst_r.at[k], at_ctx(k))
        cp.start()
        cc.append(cp)
    for cp in cc:
        cp.wait()

    def read_ctx(k):
        return tuple(
            jnp.concatenate(
                [cst[k, r, 2 * (k ^ d) : 2 * (k ^ d) + 2, :] for d in range(4)], axis=0
            )
            for r in range(3)
        )

    top, total, label = merge([got] + [read_ctx(k) for k in (1, 2, 3)])
    lt = top + jnp.log(total)
    mask_rows = []
    for d in range(4):
        toks = pl.ds(pl.multiple_of(flip(c, d) * tl, tl), tl)
        mask_rows += [auxi[0, 1:2, toks], auxi[1, 1:2, toks]]
    mk = jnp.concatenate(mask_rows, axis=0).astype(F32)
    response = lax.rem(lax.broadcasted_iota(jnp.int32, (8, tl), 0), 2)
    counted = mk * (label - lt)
    relative = []
    for s in range(2):
        part = jnp.sum(jnp.where(response == s, counted, 0.0), axis=0, keepdims=True)
        slice_sum = jnp.sum(part, axis=1, keepdims=True)
        relative.append((slice_sum + auxf[s, 0:1, 0:1]) - auxf[s, 1:2, 0:1])
    margin = beta_value * (relative[0] - relative[1])
    coef = beta_value / (1.0 + jnp.exp(margin))
    seq = jnp.where(response == 1, coef, -coef)
    ab[0] = loss_scale * mk * (2.0 * z_weight * lt - seq) * jnp.exp(st[0] - lt)
    ab[1] = loss_scale * mk * seq

    def gradient(d, s):
        u = 2 * d + s
        lanes = slice(s * tl, (s + 1) * tl)
        b = jnp.where(is_label(d, s), ab[1, u : u + 1, :], 0.0)
        g = LT[d, :, lanes] * ab[0, u : u + 1, :] + b
        GT[d, :, lanes] = g.astype(BF16)
        G[d, s] = g.T.astype(BF16)

    first, second = (1, 2), (2, 1)

    def cols(i):
        return pl.ds(pl.multiple_of(flip(zs, PARTS - 1 - i) * CW, CW), CW)

    def term(d, s, i):
        return jnp.dot(G[d, s], w[:, cols(i)], preferred_element_type=F32)

    c1, c2, cz = {}, {}, []
    second_term, own_term = {}, {}

    def send_first(i, h, responses=(0, 1)):
        hs = slice(h * hr, (h + 1) * hr)
        for s in responses:
            f = first[s]
            if h == 0:
                S1[i, s, 1] = term(3, s, i).astype(BF16)
                S1[i, s, 0] = term(f, s, i).astype(BF16)
            cp = remote(
                S1.at[i, s, :, hs], R1.at[i, s, :, hs],
                s1_s.at[i, s, h], s1_r.at[i, s, h], at_ctx(f),
            )
            cp.start()
            c1[i, s, h] = cp

    def send_second(i, h):
        hs = slice(h * hr, (h + 1) * hr)
        for s in range(2):
            g = second[s]
            if h == 0:
                second_term[s] = term(g, s, i)
            c1[i, s, h].wait_recv()
            S2[i, s, hs] = (second_term[s][hs] + R1[i, s, 1, hs].astype(F32)).astype(BF16)
            cp = remote(
                S2.at[i, s, hs], R2.at[i, s, hs], s2_s.at[i, s, h], s2_r.at[i, s, h], at_ctx(g)
            )
            cp.start()
            c2[i, s, h] = cp

    zm = lax.rem(z, m)

    def send_vocab(i, h):
        hs = slice(h * hr, (h + 1) * hr)
        for s in range(2):
            if h == 0:
                own_term[s] = term(0, s, i)
            mine = own_term[s][hs] + R1[i, s, 0, hs].astype(F32)
            c2[i, s, h].wait_recv()
            mine = mine + R2[i, s, hs].astype(F32)
            if i == PARTS - 1:
                FA[s, hs] = mine
            ZS[i, s, hs] = mine.astype(BF16)
        for k in reversed(range(m)):
            x = (PARTS - 1 - i) * m + k
            if x == 0:
                continue
            if m == 1:
                src = ZS.at[i, :, hs]
            else:
                src = ZS.at[i, :, hs, pl.ds(pl.multiple_of(flip(zm, k) * cw, cw), cw)]
            cp = remote(src, ZR.at[x, :, hs], z_s.at[x, h], z_r.at[x, h], at_vocab(x))
            cp.start()
            cz.append(cp)

    tile = 512
    head_tiles = half // tile

    def head_copy(t):
        where = pl.ds(pl.multiple_of(t * tile, tile), tile)
        return pltpu.make_async_copy(HO.at[:, where], head_out.at[:, where], ho_sem.at[t])

    def head(low, high):
        def body(t, carry):
            where = pl.ds(pl.multiple_of(t * tile, tile), tile)
            acc = jnp.zeros((rows, tile), F32)
            for d in range(4):
                acc += jnp.dot(
                    GT[d], H[d, :, :, where].reshape(2 * tl, tile), preferred_element_type=F32
                )
            HO[:, where] = acc.astype(BF16)
            head_copy(t).start()
            return carry

        lax.fori_loop(low, high, body, 0)

    gradient(3, 0)
    gradient(1, 0)
    send_first(0, 0, (0,))
    send_first(0, 1, (0,))
    gradient(3, 1)
    gradient(2, 1)
    send_first(0, 0, (1,))
    send_first(0, 1, (1,))
    for d, s in ((2, 0), (1, 1), (0, 0), (0, 1)):
        gradient(d, s)
    send_first(1, 0)
    head(0, 1)
    send_second(0, 0)
    send_first(1, 1)
    head(1, 2)
    send_second(0, 1)
    send_first(2, 0)
    head(2, 3)
    send_second(1, 0)
    send_vocab(0, 0)
    send_first(2, 1)
    head(3, 4)
    send_second(1, 1)
    send_vocab(0, 1)
    send_first(3, 0)
    head(4, 5)
    send_second(2, 0)
    send_vocab(1, 0)
    send_first(3, 1)
    head(5, 6)
    send_second(2, 1)
    send_vocab(1, 1)
    head(6, 7)
    send_second(3, 0)
    send_vocab(2, 0)
    head(7, head_tiles)
    send_second(3, 1)
    send_vocab(2, 1)
    send_vocab(3, 0)
    send_vocab(3, 1)
    own = pl.ds(0, cw) if m == 1 else pl.ds(pl.multiple_of(zm * cw, cw), cw)
    for cp in cz:
        cp.wait_recv()
    for s in range(2):
        total = FA[s, :, own]
        for x in range(1, n):
            total = total + ZR[x, s].astype(F32)
        GO[s] = total.astype(BF16)
    out = pltpu.make_async_copy(GO, gh_out, lsem.at[2])
    out.start()
    to_partner.wait_send()
    for cp in ag:
        cp.wait_send()
    for j in range(3):
        for d in (1, 2, 3):
            chain_wait_send(j, d)
    for cp in list(c1.values()) + list(c2.values()) + cz:
        cp.wait_send()

    def drain(t, carry):
        head_copy(t).wait()
        return carry

    lax.fori_loop(0, head_tiles, drain, 0)
    out.wait()


def hand_over(hid_ref, head_ref, hid_out, head_out, hid_v, head_v, in_sems, out_sems):
    rows = head_ref.shape[0]
    count = 8
    step = rows // count
    pieces = [(hid_ref, hid_v, hid_out)]
    for t in range(count):
        part = pl.ds(t * step, step)
        pieces.append((head_ref.at[part], head_v.at[part], head_out.at[part]))
    reads = [pltpu.make_async_copy(a, v, in_sems.at[t]) for t, (a, v, _) in enumerate(pieces)]
    writes = [pltpu.make_async_copy(v, o, out_sems.at[t]) for t, (_, v, o) in enumerate(pieces)]
    for cp in reads:
        cp.start()
    for cp, out in zip(reads, writes):
        cp.wait()
        out.start()
    for cp in writes:
        cp.wait()


def solution(mesh):
    n = mesh.shape["vocab"]

    def local(hidden, head_weight, labels, token_mask, other_logps, ref_logps):
        tl = hidden.shape[1]
        rows, half = head_weight.shape
        toks = labels.shape[1]
        CW, cw = half // PARTS, half // n
        vm = pltpu.VMEM
        dma = pltpu.SemaphoreType.DMA
        any_spec = pl.BlockSpec(memory_space=pl.ANY)
        vmem_spec = pl.BlockSpec(memory_space=pltpu.VMEM)
        results = pl.pallas_call(
            functools.partial(kernel, n),
            out_shape=(
                jax.ShapeDtypeStruct((2, tl, cw), BF16),
                jax.ShapeDtypeStruct((rows, half), BF16),
            ),
            in_specs=[any_spec, any_spec] + [vmem_spec] * 4,
            out_specs=(any_spec, any_spec),
            scratch_shapes=[
                vm((rows, half), BF16),
                vm((tl, half), BF16),
                vm((4, 2, tl, half), BF16),
                vm((4, rows, 2 * tl), F32),
                vm((4, rows, 2 * tl), F32),
                vm((4, rows, 2 * tl), BF16),
                vm((4, 2, tl, rows), BF16),
                vm((PARTS, 2, 2, tl, CW), BF16),
                vm((PARTS, 2, 2, tl, CW), BF16),
                vm((PARTS, 2, tl, CW), BF16),
                vm((PARTS, 2, tl, CW), BF16),
                vm((PARTS, 2, tl, CW), BF16),
                vm((n, 2, tl, cw), BF16),
                vm((2, tl, CW), F32),
                vm((rows, half), BF16),
                vm((2, tl, cw), BF16),
                vm((3, 8, tl), F32),
                vm((3, 8, tl), F32),
                vm((n, 3, 8, tl), F32),
                vm((4, 3, 8, tl), F32),
                vm((2, 8, tl), F32),
                vm((2, 8, toks), jnp.int32),
                vm((2, 8, 128), F32),
                dma((4,)),
                dma((2,)),
                dma((4,)),
                dma((4, 2)),
                dma((4, 2)),
                dma((4, 2, 2)),
                dma((4, 2, 2)),
                dma((2, 3, 4)),
                dma((2, 3, 4)),
                dma((4,)),
                dma((4,)),
                dma((n,)),
                dma((n,)),
                dma((4,)),
                dma((4,)),
                dma((PARTS, 2, 2)),
                dma((PARTS, 2, 2)),
                dma((PARTS, 2, 2)),
                dma((PARTS, 2, 2)),
                dma((n, 2)),
                dma((n, 2)),
                dma((half // 512,)),
            ],
            compiler_params=pltpu.CompilerParams(
                collective_id=0, has_side_effects=True, vmem_limit_bytes=58 * 1024 * 1024
            ),
            cost_estimate=pl.CostEstimate(
                flops=6 * 8 * tl * rows * half, bytes_accessed=6 * rows * half, transcendentals=0
            ),
        )(
            hidden, head_weight, labels, token_mask,
            other_logps.reshape(1, 1), ref_logps.reshape(1, 1),
        )
        return pl.pallas_call(
            hand_over,
            out_shape=tuple(jax.ShapeDtypeStruct(r.shape, r.dtype) for r in results),
            in_specs=[any_spec, any_spec],
            out_specs=(any_spec, any_spec),
            scratch_shapes=[vm(r.shape, r.dtype) for r in results] + [dma((9,)), dma((9,))],
            compiler_params=pltpu.CompilerParams(vmem_limit_bytes=58 * 1024 * 1024),
            cost_estimate=pl.CostEstimate(
                flops=0, bytes_accessed=4 * rows * half, transcendentals=0
            ),
        )(*results)

    return jax.shard_map(
        local,
        mesh=mesh,
        in_specs=(
            P("pair", "ctx", None),
            P(("ctx", "vocab"), "pair"),
            P("pair", None),
            P("pair", None),
            P("pair"),
            P("pair"),
        ),
        out_specs=(P(None, "ctx", ("pair", "vocab")), P(("ctx", "vocab"), "pair")),
        check_vma=False,
    )
```
